32 devices in a mesh: slab: 4 (over z), piece: 8 (over y, x, core).
Axes of the slice: x: 2, y: 2, z: 4, core: 2. Of those that a mesh axis runs over, the one named last changes fastest.
Arguments:
- fine_tiles: bfloat16 [256, 64, 512], P(('slab', 'piece')), may hold values from -0.25 to 0.25
- fine_cols: int32 [256, 8], P(('slab', 'piece')), may hold values from 0 to 23
- bond_mask: int32 [256, 8], P(('slab', 'piece')), may hold values 0 or 1
- diag_inv: bfloat16 [256, 64, 64], P(('slab', 'piece')), may hold values from -0.75 to 0.75
- tentative: bfloat16 [256, 64, 64], P(('slab', 'piece')), may hold values from -0.75 to 0.75
- aggregate: int32 [256], P(('slab', 'piece')), may hold values from 0 to 7
- tentative_two: bfloat16 [256, 64, 64], P(('slab', 'piece')), may hold values from -0.75 to 0.75
- aggregate_two: int32 [256], P(('slab', 'piece')), may hold values from 0 to 7
Outputs:
- coarse_one: float32 [256, 64, 3584], P(('slab', 'piece'))
- coarse_two: float32 [32, 64, 3584], P(('slab', 'piece'))
The draws below stay inside these ranges and needn't reach their ends.
All inputs are finite; a program needn't handle non-finite values. No bound on the sum of `bond_mask` on one device may be relied on, other than what follows from the above.
Results may differ from the reference program's by a relative error of at most 0.008.
Values may be sent and summed in bfloat16 or wider, within the bound.
A program may use at most 128 MiB of HBM per device.

```python
import jax
import jax.numpy as jnp
from jax import lax

TILE = 64
BLOCKS = 8
SLOTS = 8
AGGS = 8
FINE_ROWS = 256
AGG_ROWS = 256
TWO_SLAB = 8
N_SLAB = 4
N_PIECE = 8
DEVICES = 32


def plant(result, stream_key, low, top_value):
    index_at = [jax.random.randint(jax.random.fold_in(stream_key, axis), (), 0, length) for axis, length in enumerate(result.shape)]
    widest = result.shape.index(max(result.shape))
    beside = index_at[:widest] + [(index_at[widest] + 1) % result.shape[widest]] + index_at[widest + 1:]
    return result.at[tuple(index_at)].set(low).at[tuple(beside)].set(top_value)


def shard_levels(rng, dims, cuts, smallest, top_value):
    def one(dim, parts):
        draws = jax.random.uniform(jax.random.fold_in(jax.random.fold_in(rng, 6), dim), (parts,), jnp.float32, smallest / len(cuts), top_value / len(cuts))
        return jnp.repeat(jnp.exp(draws), dims[dim] // parts).reshape((-1,) + (1,) * (len(dims) - dim - 1))

    gain = one(*cuts[0])
    for cut in cuts[1:]:
        gain = gain * one(*cut)
    return gain


def scatter_about(rng, dims, scale, bound, split=(), held_as=jnp.bfloat16):
    array = jax.random.normal(rng, dims, jnp.float32) * scale
    if len(split) > 0:
        array = shard_levels(rng, dims, split, -0.22, 0.18) * array
    return jnp.clip(array, min=-bound, max=bound).astype(held_as)


def setup_inputs(seed: int = 0) -> dict:
    keys = jax.random.split(jax.random.key(seed), 9)
    return {
        "fine_tiles": scatter_about(keys[0], (FINE_ROWS, TILE, SLOTS * TILE), (TILE * SLOTS) ** -0.5, 0.25, ((0, 32),)),
        "fine_cols": plant(jax.random.randint(keys[1], (FINE_ROWS, SLOTS), 0, 3 * BLOCKS), jax.random.fold_in(keys[1], 1), 0, (3 * BLOCKS) - 1).astype(jnp.int32),
        "bond_mask": plant((jax.random.randint(keys[2], (FINE_ROWS, SLOTS), 0, 8) < 7).astype(jnp.int32), jax.random.fold_in(keys[2], 1), 0, 1),
        "diag_inv": scatter_about(keys[3], (FINE_ROWS, TILE, TILE), TILE ** -0.5, 0.75, ((0, 32),)),
        "tentative": scatter_about(keys[4], (FINE_ROWS, TILE, TILE), TILE ** -0.5, 0.75, ((0, 32),)),
        "aggregate": plant(jax.random.randint(keys[5], (FINE_ROWS,), 0, AGGS), jax.random.fold_in(keys[5], 1), 0, AGGS - 1).astype(jnp.int32),
        "tentative_two": scatter_about(keys[6], (AGG_ROWS, TILE, TILE), TILE ** -0.5, 0.75, ((0, 32),)),
        "aggregate_two": plant(jax.random.randint(keys[7], (AGG_ROWS,), 0, TWO_SLAB), jax.random.fold_in(keys[7], 1), 0, TWO_SLAB - 1).astype(jnp.int32),
    }


DAMPING = 2.0 / 3.0
EXACT_MODE = lax.Precision.HIGHEST


def slot_tiles(tiles, agg_ids, count):
    onehot = (agg_ids[:, None] == jnp.arange(count, dtype=jnp.int32)[None, :]).astype(jnp.float32)
    placed = tiles.astype(jnp.float32)[:, :, None, :] * onehot[:, None, :, None]
    return placed.astype(jnp.bfloat16).reshape(tiles.shape[0], tiles.shape[1], count * tiles.shape[2])


def prolong_rows(fine_tiles, fine_cols, bond_mask, diag_inv, own_slot, basis_rim):
    blocks, tile_size = diag_inv.shape[0], diag_inv.shape[1]
    slot_count = fine_cols.shape[1]
    agg_width = own_slot.shape[2]
    quad = fine_tiles.astype(jnp.float32).reshape(blocks, tile_size, slot_count, tile_size)
    smooth = jnp.einsum('irs,iskt->ikrt', diag_inv.astype(jnp.float32), quad, precision=EXACT_MODE)
    smooth = (DAMPING * bond_mask.astype(jnp.float32)[:, :, None, None] * smooth).astype(jnp.bfloat16)
    summed = jnp.zeros((blocks, tile_size, 3, agg_width), jnp.float32)
    for k in range(slot_count):
        column = fine_cols[:, k].astype(jnp.int32)
        rows_in = jnp.take(basis_rim, column, axis=0).astype(jnp.float32)
        product = jnp.einsum('irs,isq->irq', smooth[:, k].astype(jnp.float32), rows_in, precision=EXACT_MODE)
        side_mask = (column[:, None] // blocks == jnp.arange(3, dtype=jnp.int32)[None, :]).astype(jnp.float32)
        summed = summed - product[:, :, None, :] * side_mask[:, None, :, None]
    summed = summed.at[:, :, 1, :].add(own_slot.astype(jnp.float32))
    return summed.reshape(blocks, tile_size, 3 * agg_width).astype(jnp.bfloat16)


def apply_rows(fine_tiles, fine_cols, bond_mask, prolong_rim, agg_width):
    blocks, tile_size = fine_tiles.shape[0], fine_tiles.shape[1]
    slot_count = fine_cols.shape[1]
    quad = fine_tiles.astype(jnp.float32).reshape(blocks, tile_size, slot_count, tile_size)
    quad = quad * bond_mask.astype(jnp.float32)[:, None, :, None]
    sides = jnp.zeros((blocks, tile_size, 3, 3 * agg_width), jnp.float32)
    for k in range(slot_count):
        column = fine_cols[:, k].astype(jnp.int32)
        rows_in = jnp.take(prolong_rim, column, axis=0).astype(jnp.float32)
        product = jnp.einsum('irs,isq->irq', quad[:, :, k, :], rows_in, precision=EXACT_MODE)
        side_mask = (column[:, None] // blocks == jnp.arange(3, dtype=jnp.int32)[None, :]).astype(jnp.float32)
        sides = sides + product[:, :, None, :] * side_mask[:, None, :, None]
    summed = jnp.pad(sides[:, :, 0], ((0, 0), (0, 0), (0, 2 * agg_width)))
    summed = summed + jnp.pad(sides[:, :, 1], ((0, 0), (0, 0), (agg_width, agg_width)))
    summed = summed + jnp.pad(sides[:, :, 2], ((0, 0), (0, 0), (2 * agg_width, 0)))
    return summed.astype(jnp.bfloat16)


def level_partial(coarse_rows, two_tiles, two_ids, basis, groups):
    agg_count, tile_size = two_tiles.shape[0], two_tiles.shape[1]
    left = jnp.einsum('ars,arc->asc', two_tiles.astype(jnp.float32), coarse_rows, precision=EXACT_MODE)
    left = left.reshape(agg_count, tile_size, 7, agg_count, tile_size)
    right = basis.astype(jnp.float32).reshape(7, agg_count, tile_size, groups * tile_size)
    both = jnp.einsum('asobt,obtq->asoq', left, right, precision=EXACT_MODE)
    onehot = (two_ids[:, None] == jnp.arange(groups, dtype=jnp.int32)[None, :]).astype(jnp.float32)
    placed = jnp.einsum('ag,asoq->gsoq', onehot, both, precision=EXACT_MODE)
    return placed.reshape(groups, tile_size, 7 * groups * tile_size)


def reference(fine_tiles, fine_cols, bond_mask, diag_inv, tentative, aggregate, tentative_two, aggregate_two):
    slabs, groups = N_SLAB, N_PIECE
    agg_width = AGGS * TILE

    def on_grid(x, count):
        return x.reshape((slabs, groups, count) + x.shape[1:])

    def framed(x, count, depth):
        grid = on_grid(x, count)
        zero = jnp.zeros((depth,) + grid.shape[1:], grid.dtype)
        return jnp.concatenate([zero, grid, zero], 0)

    tiles_g = on_grid(fine_tiles, BLOCKS)
    cols_g = on_grid(fine_cols, BLOCKS)
    mask_g = on_grid(bond_mask, BLOCKS)
    dinv_g = on_grid(diag_inv, BLOCKS)
    qslot = slot_tiles(tentative, aggregate, AGGS)
    qslot_g = on_grid(qslot, BLOCKS)
    qpad = framed(qslot, BLOCKS, 1)

    def first(index):
        s = index // groups
        p = index % groups
        rim = jnp.concatenate([qpad[s, p], qpad[s + 1, p], qpad[s + 2, p]], 0)
        return prolong_rows(tiles_g[s, p], cols_g[s, p], mask_g[s, p], dinv_g[s, p], qslot_g[s, p], rim)

    device_ids = jnp.arange(DEVICES, dtype=jnp.int32)
    prolong = lax.map(first, device_ids)
    prolong_flat = prolong.reshape(DEVICES * BLOCKS, TILE, 3 * agg_width)
    ppad = framed(prolong_flat, BLOCKS, 1)

    def second(index):
        s = index // groups
        p = index % groups
        rim = jnp.concatenate([ppad[s, p], ppad[s + 1, p], ppad[s + 2, p]], 0)
        applied = apply_rows(tiles_g[s, p], cols_g[s, p], mask_g[s, p], rim, agg_width)
        own = prolong[index].astype(jnp.float32).reshape(BLOCKS * TILE, 3 * agg_width)
        right = applied.astype(jnp.float32).reshape(BLOCKS * TILE, 5 * agg_width)
        product = lax.dot_general(own, right, (((0,), (0,)), ((), ())), precision=EXACT_MODE)
        return product.reshape(3, AGGS, TILE, 5 * agg_width)

    rowsets = lax.map(second, device_ids).reshape(slabs, groups, 3, AGGS, TILE, 5 * agg_width)
    zero_slab = jnp.zeros((1, groups, AGGS, TILE, 5 * agg_width), jnp.float32)
    from_next = jnp.concatenate([rowsets[1:, :, 0], zero_slab], 0)
    from_prev = jnp.concatenate([zero_slab, rowsets[:-1, :, 2]], 0)
    coarse = jnp.pad(rowsets[:, :, 1], ((0, 0), (0, 0), (0, 0), (0, 0), (agg_width, agg_width)))
    coarse = coarse + jnp.pad(from_next, ((0, 0), (0, 0), (0, 0), (0, 0), (2 * agg_width, 0)))
    coarse = coarse + jnp.pad(from_prev, ((0, 0), (0, 0), (0, 0), (0, 0), (0, 2 * agg_width)))
    coarse_one = coarse.reshape(DEVICES * AGGS, TILE, 7 * agg_width)

    q2slot = slot_tiles(tentative_two, aggregate_two, groups)
    q2pad = framed(q2slot, AGGS, 3)
    two_g = on_grid(tentative_two, AGGS)
    ids_g = on_grid(aggregate_two, AGGS)

    def slab_sum(s):
        def add_piece(p, summed):
            basis = jnp.concatenate([q2pad[s + j, p] for j in range(7)], 0)
            term = level_partial(coarse[s, p], two_g[s, p], ids_g[s, p], basis, groups)
            term = lax.optimization_barrier(term.astype(jnp.bfloat16)).astype(jnp.float32)
            return summed + term

        start = jnp.zeros((groups, TILE, 7 * groups * TILE), jnp.float32)
        return lax.fori_loop(0, groups, add_piece, start)

    level_two = lax.map(slab_sum, jnp.arange(slabs, dtype=jnp.int32))
    coarse_two = level_two.reshape(slabs * groups, TILE, 7 * groups * TILE)
    return (coarse_one, coarse_two)
```

```python
import functools

import jax
import jax.numpy as jnp
from jax import lax
from jax.experimental import pallas as pl
from jax.experimental.pallas import tpu as pltpu
from jax.sharding import PartitionSpec as P

DAMPING = 2.0 / 3.0
LANES = 128
MESH = pl.DeviceIdType.MESH
VMEM_LIMIT = 56 * 1024 * 1024
F32 = jnp.float32
BF16 = jnp.bfloat16


def mm(a, b):
    return jnp.dot(a, b, preferred_element_type=F32)


def gather_kernel(n, far, a_ref, d_ref, t_ref, q_ref, i_ref, ag, dg, tg, ig, send_sem, recv_sem):
    s, p = lax.axis_index("slab"), lax.axis_index("piece")
    barrier = pltpu.get_barrier_semaphore()

    @pl.when(s > 0)
    def _():
        pl.semaphore_signal(barrier, inc=1, device_id=(s - 1, p), device_id_type=MESH)

    @pl.when(s < n - 1)
    def _():
        pl.semaphore_signal(barrier, inc=1, device_id=(s + 1, p), device_id_type=MESH)

    half = d_ref.shape[0] // 2
    ag[s] = a_ref[...]
    dg[s] = jnp.concatenate([d_ref[0:half, :], d_ref[half : 2 * half, :]], axis=1)
    tg[s] = jnp.concatenate([t_ref[...], q_ref[...]], axis=1)
    ig[s] = i_ref[...]

    peers = jnp.where(s > 0, 1, 0) + jnp.where(s < n - 1, 1, 0)
    pl.semaphore_wait(barrier, peers)

    arrays = (ig, tg, dg, ag)
    reach = (far, far, 2, 2)

    def copy(way, step, which, slab):
        there = s + 1 if way == 0 else s - 1
        return pltpu.make_async_remote_copy(
            src_ref=arrays[which].at[slab],
            dst_ref=arrays[which].at[slab],
            send_sem=send_sem.at[way, step, which],
            recv_sem=recv_sem.at[way, step, which],
            device_id=(there, p),
            device_id_type=MESH,
        )

    def sends(way, step):
        if way == 0:
            return (s - step >= 0) & (s + 1 < n), s - step
        return (s + step < n) & (s >= 1), s + step

    def gets(way, step):
        if way == 0:
            return s - 1 - step >= 0, s - 1 - step
        return s + 1 + step < n, s + 1 + step

    steps = min(far, n - 1)
    for step in range(steps + 1):
        for which in range(4):
            for way in range(2):
                if 0 < step <= min(reach[which], steps):
                    ok, slab = gets(way, step - 1)

                    @pl.when(ok)
                    def _(way=way, which=which, slab=slab):
                        copy(way, step - 1, which, slab).wait_recv()

                if step < min(reach[which], steps):
                    ok, slab = sends(way, step)

                    @pl.when(ok)
                    def _(way=way, which=which, slab=slab):
                        copy(way, step, which, slab).start()

    for step in range(steps):
        for which in range(4):
            for way in range(2):
                if step < reach[which]:
                    ok, slab = sends(way, step)

                    @pl.when(ok)
                    def _(way=way, which=which, slab=slab):
                        copy(way, step, which, slab).wait_send()


def level_kernel(
    n, blocks, slots, aggs, groups, tile, s_ref, i_ref, ag, dg, tg,
    out, cb, t2s, t2t, ad, sd, pro, ts, acc, bd, wm,
):
    s = s_ref[0]
    rows, w, gw = blocks * tile, aggs * tile, groups * tile
    pair = 2 * tile
    lane = lax.broadcasted_iota(jnp.int32, (tile, pair), 1) // tile

    for v in range(n):
        near = jnp.abs(v - s) <= 3
        for b in range(blocks):
            x = tg[v, b * tile : (b + 1) * tile, :].astype(F32)
            turned = pltpu.roll(x, tile, 1)
            one = jnp.where(lane == 0, x, turned)
            two = jnp.where(lane == 0, turned, x)
            g1 = jnp.where(near, i_ref[v, 2, b], -1)
            g2 = jnp.where(near, i_ref[v, 3, b], -1)
            for q in range(w // pair):
                ts[v, b * tile : (b + 1) * tile, q * pair : (q + 1) * pair] = jnp.where(
                    lane + 2 * q == g1, one, 0.0
                ).astype(BF16)
            for q in range(gw // pair):
                t2s[v, b * tile : (b + 1) * tile, q * pair : (q + 1) * pair] = jnp.where(
                    lane + 2 * q == g2, two, 0.0
                ).astype(BF16)

    t2t[...] = t2s[s].astype(F32).T.astype(BF16)
    bd[...] = jnp.zeros_like(bd)

    for e in range(-2, 3):
        u = s + e

        @pl.when((u >= 0) & (u < n))
        def _(e=e, u=u):
            def row(i, carry):
                acc[...] = jnp.zeros_like(acc)
                base = pl.multiple_of(i * tile, tile)
                for k2 in range(slots // 2):
                    x = ag[u, pl.ds(base, tile), k2 * pair : (k2 + 1) * pair].astype(F32)
                    turned = pltpu.roll(x, tile, 1)
                    for odd in range(2):
                        k = 2 * k2 + odd
                        c = i_ref[u, 0, i * slots + k]
                        m = i_ref[u, 1, i * slots + k]
                        side = lax.rem(c, 2)
                        y = jnp.where(side == odd, x, turned)
                        keep = jnp.where(m != 0, side, -1)
                        at = pl.multiple_of((c // 2) * pair, pair)
                        acc[:, pl.ds(at, pair)] += jnp.where(lane == keep, y, 0.0)
                ad[e + 2, pl.ds(base, tile), :] = acc[...].astype(BF16)
                return carry

            lax.fori_loop(0, blocks, row, 0)
            half = blocks // 2
            for h in range(2):
                for b in range(half):
                    x = dg[u, b * tile : (b + 1) * tile, :].astype(F32)
                    if b % 2 != h:
                        x = pltpu.roll(x, tile, 1)
                    bd[b * tile : (b + 1) * tile, (b // 2) * pair : (b // 2 + 1) * pair] = (
                        jnp.where(lane == b % 2, x, 0.0).astype(BF16)
                    )
                lo = h * half * tile
                hi = lo + half * tile
                sd[lo:hi, :] = (DAMPING * mm(bd[...], ad[e + 2, lo:hi, :])).astype(BF16)
            for j in range(3):
                v = u + j - 1
                inside = (v >= 0) & (v < n)

                @pl.when(inside)
                def _(j=j, v=v):
                    value = -mm(sd[:, j * rows : (j + 1) * rows], ts[v])
                    if j == 1:
                        value = value + ts[v].astype(F32)
                    pro[e + 2, :, j * w : (j + 1) * w] = value.astype(BF16)

                @pl.when(jnp.logical_not(inside))
                def _(j=j):
                    pro[e + 2, :, j * w : (j + 1) * w] = jnp.zeros((rows, w), BF16)

        @pl.when((u < 0) | (u >= n))
        def _(e=e):
            pro[e + 2] = jnp.zeros((rows, 3 * w), BF16)
            if abs(e) < 2:
                ad[e + 2] = jnp.zeros((rows, 3 * rows), BF16)

    turned = [pro[dj + 2, :, (1 - dj) * w : (2 - dj) * w].astype(F32).T.astype(BF16) for dj in (-1, 0, 1)]
    for e in range(-2, 3):
        total = None
        for dj in (-1, 0, 1):
            j = e - dj + 1
            if 0 <= j < 3:
                term = mm(turned[dj + 1], ad[dj + 2, :, j * rows : (j + 1) * rows])
                total = term if total is None else total + term
        wm[e + 2] = total.astype(BF16)

    short = n < 7
    for f in range(-3, 4):
        t = s + f
        inside = (t >= 0) & (t < n)

        @pl.when(inside)
        def _(f=f, t=t):
            total = None
            for e in range(max(-2, f - 1), min(2, f + 1) + 1):
                j = f - e + 1
                term = mm(wm[e + 2], pro[e + 2, :, j * w : (j + 1) * w])
                total = term if total is None else total + term
            out[:, (f + 3) * w : (f + 4) * w] = total
            cb[t if short else f + 3] = total.astype(BF16)

        @pl.when(jnp.logical_not(inside))
        def _(f=f):
            out[:, (f + 3) * w : (f + 4) * w] = jnp.zeros((w, w), F32)
            if not short:
                cb[f + 3] = jnp.zeros((w, w), BF16)


def scatter_kernel(
    n, parts, groups, tile, cb, t2s, t2t, out, term, mine, rx1, tx2, rx2,
    send1, recv1, send2, recv2,
):
    s, p = lax.axis_index("slab"), lax.axis_index("piece")
    chips = groups // 2
    odd = lax.rem(p, 2)
    chip = p // 2
    sibling = p + 1 - 2 * odd
    gw = groups * tile
    mates = [2 * lax.rem(chip + o, chips) + odd for o in range(1, chips)]

    barrier = pltpu.get_barrier_semaphore()
    for mate in [sibling] + mates:
        pl.semaphore_signal(barrier, inc=1, device_id=(s, mate), device_id_type=MESH)
    if n < 7:
        out[...] = jnp.zeros_like(out)
    pl.semaphore_wait(barrier, chips)

    def pair_copy(m):
        return pltpu.make_async_remote_copy(
            src_ref=term.at[m, 1 - odd],
            dst_ref=rx1.at[m],
            send_sem=send1.at[m],
            recv_sem=recv1.at[m],
            device_id=(s, sibling),
            device_id_type=MESH,
        )

    def chip_copy(m, o):
        return pltpu.make_async_remote_copy(
            src_ref=tx2.at[m, o - 1],
            dst_ref=rx2.at[m, o - 1],
            send_sem=send2.at[m, o - 1],
            recv_sem=recv2.at[m, o - 1],
            device_id=(s, mates[o - 1]),
            device_id_type=MESH,
        )

    def pair_sum(m):
        pair_copy(m).wait_recv()
        for o in range(1, chips):
            h = lax.rem(chip + o, chips)
            tx2[m, o - 1] = (term[m, odd, h].astype(F32) + rx1[m, h].astype(F32)).astype(BF16)
            chip_copy(m, o).start()
        mine[m] = term[m, odd, chip].astype(F32) + rx1[m, chip].astype(F32)

    for m in range(parts):
        v = m if n < 7 else jnp.clip(s + m - 3, 0, n - 1)
        left = mm(t2t[...], cb[m]).astype(BF16)
        both = mm(left, t2s[v]).astype(BF16)
        for g in range(groups):
            term[m, g % 2, g // 2] = both[g * tile : (g + 1) * tile, :]
        pair_copy(m).start()
        if m > 0:
            pair_sum(m - 1)
    pair_sum(parts - 1)
    for m in range(parts):
        total = mine[m]
        for o in range(1, chips):
            chip_copy(m, o).wait_recv()
            total = total + rx2[m, o - 1].astype(F32)
        place = (m + 3 - s) * gw if n < 7 else m * gw
        out[:, pl.ds(pl.multiple_of(place, LANES), gw)] = total
    for m in range(parts):
        pair_copy(m).wait_send()
        for o in range(1, chips):
            chip_copy(m, o).wait_send()


def per_device(
    fine_tiles, fine_cols, bond_mask, diag_inv, tentative, aggregate, tentative_two, aggregate_two
):
    blocks, tile = diag_inv.shape[0], diag_inv.shape[1]
    slots = fine_cols.shape[1]
    aggs = tentative_two.shape[0]
    n, groups = lax.axis_size("slab"), lax.axis_size("piece")
    rows, w, gw = blocks * tile, aggs * tile, groups * tile
    parts = min(7, n)
    vmem = pl.BlockSpec(memory_space=pltpu.VMEM)
    smem = pl.BlockSpec(memory_space=pltpu.SMEM)
    shape = jax.ShapeDtypeStruct

    width = -(-blocks * slots // LANES) * LANES

    def line(x):
        x = x.reshape(1, -1)
        return jnp.pad(x, ((0, 0), (0, width - x.shape[1])))

    ints = jnp.concatenate([line(fine_cols), line(bond_mask), line(aggregate), line(aggregate_two)], 0)
    ints = jnp.pad(ints, ((0, 4), (0, 0)))

    far = min(3, n - 1)
    ag, dg, tg, ig = pl.pallas_call(
        functools.partial(gather_kernel, n, far),
        out_shape=(
            shape((n, rows, slots * tile), BF16),
            shape((n, rows // 2, 2 * tile), BF16),
            shape((n, rows, 2 * tile), BF16),
            shape((n, 8, width), jnp.int32),
        ),
        in_specs=[vmem] * 5,
        out_specs=(vmem,) * 4,
        scratch_shapes=[
            pltpu.SemaphoreType.DMA((2, far, 4)),
            pltpu.SemaphoreType.DMA((2, far, 4)),
        ],
        compiler_params=pltpu.CompilerParams(
            collective_id=0, has_side_effects=True, vmem_limit_bytes=VMEM_LIMIT
        ),
    )(
        fine_tiles.reshape(rows, slots * tile),
        diag_inv.reshape(rows, tile),
        tentative.reshape(rows, tile),
        tentative_two.reshape(w, tile),
        ints,
    )

    slab = lax.axis_index("slab").astype(jnp.int32).reshape(1)
    coarse, cb, t2s, t2t = pl.pallas_call(
        functools.partial(level_kernel, n, blocks, slots, aggs, groups, tile),
        out_shape=(
            shape((w, 7 * w), F32),
            shape((parts, w, w), BF16),
            shape((n, w, gw), BF16),
            shape((gw, w), BF16),
        ),
        in_specs=[smem, smem, vmem, vmem, vmem],
        out_specs=(vmem,) * 4,
        scratch_shapes=[
            pltpu.VMEM((5, rows, 3 * rows), BF16),
            pltpu.VMEM((rows, 3 * rows), BF16),
            pltpu.VMEM((5, rows, 3 * w), BF16),
            pltpu.VMEM((n, rows, w), BF16),
            pltpu.VMEM((tile, 3 * rows), F32),
            pltpu.VMEM((rows // 2, rows // 2), BF16),
            pltpu.VMEM((5, w, rows), BF16),
        ],
        compiler_params=pltpu.CompilerParams(vmem_limit_bytes=VMEM_LIMIT),
    )(slab, ig, ag, dg, tg)

    chips = groups // 2
    level_two = pl.pallas_call(
        functools.partial(scatter_kernel, n, parts, groups, tile),
        out_shape=shape((tile, 7 * gw), F32),
        in_specs=[vmem] * 3,
        out_specs=vmem,
        scratch_shapes=[
            pltpu.VMEM((parts, 2, chips, tile, gw), BF16),
            pltpu.VMEM((parts, tile, gw), F32),
            pltpu.VMEM((parts, chips, tile, gw), BF16),
            pltpu.VMEM((parts, chips - 1, tile, gw), BF16),
            pltpu.VMEM((parts, chips - 1, tile, gw), BF16),
            pltpu.SemaphoreType.DMA((parts,)),
            pltpu.SemaphoreType.DMA((parts,)),
            pltpu.SemaphoreType.DMA((parts, chips - 1)),
            pltpu.SemaphoreType.DMA((parts, chips - 1)),
        ],
        compiler_params=pltpu.CompilerParams(
            collective_id=1, has_side_effects=True, vmem_limit_bytes=VMEM_LIMIT
        ),
    )(cb, t2s, t2t)

    return (coarse.reshape(aggs, tile, 7 * w), level_two.reshape(1, tile, 7 * gw))


def solution(mesh):
    placed = (
        P(("slab", "piece"), None, None),
        P(("slab", "piece"), None),
        P(("slab", "piece"), None),
        P(("slab", "piece"), None, None),
        P(("slab", "piece"), None, None),
        P(("slab", "piece")),
        P(("slab", "piece"), None, None),
        P(("slab", "piece")),
    )
    return jax.shard_map(
        per_device,
        mesh=mesh,
        in_specs=placed,
        out_specs=(P(("slab", "piece"), None, None), P(("slab", "piece"), None, None)),
        check_vma=False,
    )
```

```python
import functools

import jax
import jax.numpy as jnp
import numpy as np
from jax import lax
from jax.experimental import pallas as pl
from jax.experimental.pallas import tpu as pltpu
from jax.sharding import PartitionSpec as P

DAMPING = 2.0 / 3.0
LANES = 128
MESH = pl.DeviceIdType.MESH
VMEM_LIMIT = 60 * 1024 * 1024
FUSED_LIMIT = 50 * 1024 * 1024
F32 = jnp.float32
BF16 = jnp.bfloat16


def mm(a, b):
    return jnp.dot(a, b, preferred_element_type=F32)


def gather_kernel(n, far, a_ref, d_ref, t_ref, q_ref, i_ref, ag, dg, tg, ig, send_sem, recv_sem):
    s, p = lax.axis_index("slab"), lax.axis_index("piece")
    barrier = pltpu.get_barrier_semaphore()

    @pl.when(s > 0)
    def _():
        pl.semaphore_signal(barrier, inc=1, device_id=(s - 1, p), device_id_type=MESH)

    @pl.when(s < n - 1)
    def _():
        pl.semaphore_signal(barrier, inc=1, device_id=(s + 1, p), device_id_type=MESH)

    half = d_ref.shape[0] // 2
    ag[s] = a_ref[...]
    dg[s] = jnp.concatenate([d_ref[0:half, :], d_ref[half : 2 * half, :]], axis=1)
    tg[s] = jnp.concatenate([t_ref[...], q_ref[...]], axis=1)
    ig[s] = i_ref[...]

    peers = jnp.where(s > 0, 1, 0) + jnp.where(s < n - 1, 1, 0)
    pl.semaphore_wait(barrier, peers)

    arrays = (ig, tg, dg, ag)
    reach = (far, far, 2, 2)

    def copy(way, step, which, slab):
        there = s + 1 if way == 0 else s - 1
        return pltpu.make_async_remote_copy(
            src_ref=arrays[which].at[slab],
            dst_ref=arrays[which].at[slab],
            send_sem=send_sem.at[way, step, which],
            recv_sem=recv_sem.at[way, step, which],
            device_id=(there, p),
            device_id_type=MESH,
        )

    def sends(way, step):
        if way == 0:
            return (s - step >= 0) & (s + 1 < n), s - step
        return (s + step < n) & (s >= 1), s + step

    def gets(way, step):
        if way == 0:
            return s - 1 - step >= 0, s - 1 - step
        return s + 1 + step < n, s + 1 + step

    steps = min(far, n - 1)
    for step in range(steps + 1):
        for which in range(4):
            for way in range(2):
                if 0 < step <= min(reach[which], steps):
                    ok, slab = gets(way, step - 1)

                    @pl.when(ok)
                    def _(way=way, which=which, slab=slab):
                        copy(way, step - 1, which, slab).wait_recv()

                if step < min(reach[which], steps):
                    ok, slab = sends(way, step)

                    @pl.when(ok)
                    def _(way=way, which=which, slab=slab):
                        copy(way, step, which, slab).start()

    for step in range(steps):
        for which in range(4):
            for way in range(2):
                if step < reach[which]:
                    ok, slab = sends(way, step)

                    @pl.when(ok)
                    def _(way=way, which=which, slab=slab):
                        copy(way, step, which, slab).wait_send()


def level_kernel(
    n, blocks, slots, aggs, groups, tile, s_ref, i_ref, ag, dg, tg,
    out, cb, t2s, t2t, ad, sd, pro, ts, acc, bd, wm,
):
    s = s_ref[0]
    rows, w, gw = blocks * tile, aggs * tile, groups * tile
    pair = 2 * tile
    lane = lax.broadcasted_iota(jnp.int32, (tile, pair), 1) // tile

    for v in range(n):
        near = jnp.abs(v - s) <= 3
        for b in range(blocks):
            x = tg[v, b * tile : (b + 1) * tile, :].astype(F32)
            turned = pltpu.roll(x, tile, 1)
            one = jnp.where(lane == 0, x, turned)
            two = jnp.where(lane == 0, turned, x)
            g1 = jnp.where(near, i_ref[v, 2, b], -1)
            g2 = jnp.where(near, i_ref[v, 3, b], -1)
            for q in range(w // pair):
                ts[v, b * tile : (b + 1) * tile, q * pair : (q + 1) * pair] = jnp.where(
                    lane + 2 * q == g1, one, 0.0
                ).astype(BF16)
            for q in range(gw // pair):
                t2s[v, b * tile : (b + 1) * tile, q * pair : (q + 1) * pair] = jnp.where(
                    lane + 2 * q == g2, two, 0.0
                ).astype(BF16)

    t2t[...] = t2s[s].astype(F32).T.astype(BF16)
    bd[...] = jnp.zeros_like(bd)

    for e in range(-2, 3):
        u = s + e

        @pl.when((u >= 0) & (u < n))
        def _(e=e, u=u):
            def row(i, carry):
                acc[...] = jnp.zeros_like(acc)
                base = pl.multiple_of(i * tile, tile)
                for k2 in range(slots // 2):
                    x = ag[u, pl.ds(base, tile), k2 * pair : (k2 + 1) * pair].astype(F32)
                    turned = pltpu.roll(x, tile, 1)
                    for odd in range(2):
                        k = 2 * k2 + odd
                        c = i_ref[u, 0, i * slots + k]
                        m = i_ref[u, 1, i * slots + k]
                        side = lax.rem(c, 2)
                        y = jnp.where(side == odd, x, turned)
                        keep = jnp.where(m != 0, side, -1)
                        at = pl.multiple_of((c // 2) * pair, pair)
                        acc[:, pl.ds(at, pair)] += jnp.where(lane == keep, y, 0.0)
                ad[e + 2, pl.ds(base, tile), :] = acc[...].astype(BF16)
                return carry

            lax.fori_loop(0, blocks, row, 0)
            half = blocks // 2
            for h in range(2):
                for b in range(half):
                    x = dg[u, b * tile : (b + 1) * tile, :].astype(F32)
                    if b % 2 != h:
                        x = pltpu.roll(x, tile, 1)
                    bd[b * tile : (b + 1) * tile, (b // 2) * pair : (b // 2 + 1) * pair] = (
                        jnp.where(lane == b % 2, x, 0.0).astype(BF16)
                    )
                lo = h * half * tile
                hi = lo + half * tile
                sd[lo:hi, :] = (DAMPING * mm(bd[...], ad[e + 2, lo:hi, :])).astype(BF16)
            for j in range(3):
                v = u + j - 1
                inside = (v >= 0) & (v < n)

                @pl.when(inside)
                def _(j=j, v=v):
                    value = -mm(sd[:, j * rows : (j + 1) * rows], ts[v])
                    if j == 1:
                        value = value + ts[v].astype(F32)
                    pro[e + 2, :, j * w : (j + 1) * w] = value.astype(BF16)

                @pl.when(jnp.logical_not(inside))
                def _(j=j):
                    pro[e + 2, :, j * w : (j + 1) * w] = jnp.zeros((rows, w), BF16)

        @pl.when((u < 0) | (u >= n))
        def _(e=e):
            pro[e + 2] = jnp.zeros((rows, 3 * w), BF16)
            if abs(e) < 2:
                ad[e + 2] = jnp.zeros((rows, 3 * rows), BF16)

    turned = [pro[dj + 2, :, (1 - dj) * w : (2 - dj) * w].astype(F32).T.astype(BF16) for dj in (-1, 0, 1)]
    for e in range(-2, 3):
        total = None
        for dj in (-1, 0, 1):
            j = e - dj + 1
            if 0 <= j < 3:
                term = mm(turned[dj + 1], ad[dj + 2, :, j * rows : (j + 1) * rows])
                total = term if total is None else total + term
        wm[e + 2] = total.astype(BF16)

    short = n < 7
    for f in range(-3, 4):
        t = s + f
        inside = (t >= 0) & (t < n)

        @pl.when(inside)
        def _(f=f, t=t):
            total = None
            for e in range(max(-2, f - 1), min(2, f + 1) + 1):
                j = f - e + 1
                term = mm(wm[e + 2], pro[e + 2, :, j * w : (j + 1) * w])
                total = term if total is None else total + term
            out[:, (f + 3) * w : (f + 4) * w] = total
            cb[t if short else f + 3] = total.astype(BF16)

        @pl.when(jnp.logical_not(inside))
        def _(f=f):
            out[:, (f + 3) * w : (f + 4) * w] = jnp.zeros((w, w), F32)
            if not short:
                cb[f + 3] = jnp.zeros((w, w), BF16)


def scatter_kernel(
    n, parts, groups, tile, cb, t2s, t2t, out, term, mine, rx1, tx2, rx2,
    send1, recv1, send2, recv2,
):
    s, p = lax.axis_index("slab"), lax.axis_index("piece")
    chips = groups // 2
    odd = lax.rem(p, 2)
    chip = p // 2
    sibling = p + 1 - 2 * odd
    gw = groups * tile
    mates = [2 * lax.rem(chip + o, chips) + odd for o in range(1, chips)]

    barrier = pltpu.get_barrier_semaphore()
    for mate in [sibling] + mates:
        pl.semaphore_signal(barrier, inc=1, device_id=(s, mate), device_id_type=MESH)
    if n < 7:
        out[...] = jnp.zeros_like(out)
    pl.semaphore_wait(barrier, chips)

    def pair_copy(m):
        return pltpu.make_async_remote_copy(
            src_ref=term.at[m, 1 - odd],
            dst_ref=rx1.at[m],
            send_sem=send1.at[m],
            recv_sem=recv1.at[m],
            device_id=(s, sibling),
            device_id_type=MESH,
        )

    def chip_copy(m, o):
        return pltpu.make_async_remote_copy(
            src_ref=tx2.at[m, o - 1],
            dst_ref=rx2.at[m, o - 1],
            send_sem=send2.at[m, o - 1],
            recv_sem=recv2.at[m, o - 1],
            device_id=(s, mates[o - 1]),
            device_id_type=MESH,
        )

    def pair_sum(m):
        pair_copy(m).wait_recv()
        for o in range(1, chips):
            h = lax.rem(chip + o, chips)
            tx2[m, o - 1] = (term[m, odd, h].astype(F32) + rx1[m, h].astype(F32)).astype(BF16)
            chip_copy(m, o).start()
        mine[m] = term[m, odd, chip].astype(F32) + rx1[m, chip].astype(F32)

    for m in range(parts):
        v = m if n < 7 else jnp.clip(s + m - 3, 0, n - 1)
        left = mm(t2t[...], cb[m]).astype(BF16)
        both = mm(left, t2s[v]).astype(BF16)
        for g in range(groups):
            term[m, g % 2, g // 2] = both[g * tile : (g + 1) * tile, :]
        pair_copy(m).start()
        if m > 0:
            pair_sum(m - 1)
    pair_sum(parts - 1)
    for m in range(parts):
        total = mine[m]
        for o in range(1, chips):
            chip_copy(m, o).wait_recv()
            total = total + rx2[m, o - 1].astype(F32)
        place = (m + 3 - s) * gw if n < 7 else m * gw
        out[:, pl.ds(pl.multiple_of(place, LANES), gw)] = total
    for m in range(parts):
        pair_copy(m).wait_send()
        for o in range(1, chips):
            chip_copy(m, o).wait_send()


def in_stages(
    fine_tiles, fine_cols, bond_mask, diag_inv, tentative, aggregate, tentative_two, aggregate_two
):
    blocks, tile = diag_inv.shape[0], diag_inv.shape[1]
    slots = fine_cols.shape[1]
    aggs = tentative_two.shape[0]
    n, groups = lax.axis_size("slab"), lax.axis_size("piece")
    rows, w, gw = blocks * tile, aggs * tile, groups * tile
    parts = min(7, n)
    vmem = pl.BlockSpec(memory_space=pltpu.VMEM)
    smem = pl.BlockSpec(memory_space=pltpu.SMEM)
    shape = jax.ShapeDtypeStruct

    width = -(-blocks * slots // LANES) * LANES

    def line(x):
        x = x.reshape(1, -1)
        return jnp.pad(x, ((0, 0), (0, width - x.shape[1])))

    ints = jnp.concatenate([line(fine_cols), line(bond_mask), line(aggregate), line(aggregate_two)], 0)
    ints = jnp.pad(ints, ((0, 4), (0, 0)))

    far = min(3, n - 1)
    ag, dg, tg, ig = pl.pallas_call(
        functools.partial(gather_kernel, n, far),
        out_shape=(
            shape((n, rows, slots * tile), BF16),
            shape((n, rows // 2, 2 * tile), BF16),
            shape((n, rows, 2 * tile), BF16),
            shape((n, 8, width), jnp.int32),
        ),
        in_specs=[vmem] * 5,
        out_specs=(vmem,) * 4,
        scratch_shapes=[
            pltpu.SemaphoreType.DMA((2, far, 4)),
            pltpu.SemaphoreType.DMA((2, far, 4)),
        ],
        compiler_params=pltpu.CompilerParams(
            collective_id=0, has_side_effects=True, vmem_limit_bytes=VMEM_LIMIT
        ),
    )(
        fine_tiles.reshape(rows, slots * tile),
        diag_inv.reshape(rows, tile),
        tentative.reshape(rows, tile),
        tentative_two.reshape(w, tile),
        ints,
    )

    slab = lax.axis_index("slab").astype(jnp.int32).reshape(1)
    coarse, cb, t2s, t2t = pl.pallas_call(
        functools.partial(level_kernel, n, blocks, slots, aggs, groups, tile),
        out_shape=(
            shape((w, 7 * w), F32),
            shape((parts, w, w), BF16),
            shape((n, w, gw), BF16),
            shape((gw, w), BF16),
        ),
        in_specs=[smem, smem, vmem, vmem, vmem],
        out_specs=(vmem,) * 4,
        scratch_shapes=[
            pltpu.VMEM((5, rows, 3 * rows), BF16),
            pltpu.VMEM((rows, 3 * rows), BF16),
            pltpu.VMEM((5, rows, 3 * w), BF16),
            pltpu.VMEM((n, rows, w), BF16),
            pltpu.VMEM((tile, 3 * rows), F32),
            pltpu.VMEM((rows // 2, rows // 2), BF16),
            pltpu.VMEM((5, w, rows), BF16),
        ],
        compiler_params=pltpu.CompilerParams(vmem_limit_bytes=VMEM_LIMIT),
    )(slab, ig, ag, dg, tg)

    chips = groups // 2
    level_two = pl.pallas_call(
        functools.partial(scatter_kernel, n, parts, groups, tile),
        out_shape=shape((tile, 7 * gw), F32),
        in_specs=[vmem] * 3,
        out_specs=vmem,
        scratch_shapes=[
            pltpu.VMEM((parts, 2, chips, tile, gw), BF16),
            pltpu.VMEM((parts, tile, gw), F32),
            pltpu.VMEM((parts, chips, tile, gw), BF16),
            pltpu.VMEM((parts, chips - 1, tile, gw), BF16),
            pltpu.VMEM((parts, chips - 1, tile, gw), BF16),
            pltpu.SemaphoreType.DMA((parts,)),
            pltpu.SemaphoreType.DMA((parts,)),
            pltpu.SemaphoreType.DMA((parts, chips - 1)),
            pltpu.SemaphoreType.DMA((parts, chips - 1)),
        ],
        compiler_params=pltpu.CompilerParams(
            collective_id=1, has_side_effects=True, vmem_limit_bytes=VMEM_LIMIT
        ),
    )(cb, t2s, t2t)

    return (coarse.reshape(aggs, tile, 7 * w), level_two.reshape(1, tile, 7 * gw))


def whole_kernel(
    n, blocks, slots, aggs, groups, tile,
    a_ref, d_ref, t_ref, q_ref, c_ref, out, two,
    ag, dg, tg, cg, ad, sd, pro, ts, t2s, t2t, hot, bd, wm, cf, term, mine, rx1, tx2, rx2,
    send_sem, recv_sem, out_sem, send1, recv1, send2, recv2,
):
    s, p = lax.axis_index("slab"), lax.axis_index("piece")
    far = min(3, n - 1)
    rows, w, gw = blocks * tile, aggs * tile, groups * tile
    pair, half = 2 * tile, blocks // 2
    chips = groups // 2
    odd, chip = lax.rem(p, 2), p // 2
    sibling = p + 1 - 2 * odd
    mates = [2 * lax.rem(chip + o, chips) + odd for o in range(1, chips)]
    barrier = pltpu.get_barrier_semaphore()

    @pl.when(s > 0)
    def _():
        pl.semaphore_signal(barrier, inc=1, device_id=(s - 1, p), device_id_type=MESH)

    @pl.when(s < n - 1)
    def _():
        pl.semaphore_signal(barrier, inc=1, device_id=(s + 1, p), device_id_type=MESH)

    for mate in [sibling] + mates:
        pl.semaphore_signal(barrier, inc=1, device_id=(s, mate), device_id_type=MESH)

    cg[s] = c_ref[...]
    tg[s] = jnp.concatenate([t_ref[...], q_ref[...]], axis=1)
    dg[s] = jnp.concatenate([d_ref[0 : rows // 2, :], d_ref[rows // 2 : rows, :]], axis=1)
    ag[s] = a_ref[...]
    peers = chips + jnp.where(s > 0, 1, 0) + jnp.where(s < n - 1, 1, 0)
    pl.semaphore_wait(barrier, peers)

    arrays = (cg, tg, dg, ag)
    reach = (far, far, min(2, far), min(2, far))

    def valid(e):
        return (s + e >= 0) & (s + e < n)

    def copy(way, step, which, slab):
        return pltpu.make_async_remote_copy(
            src_ref=arrays[which].at[slab],
            dst_ref=arrays[which].at[slab],
            send_sem=send_sem.at[way, step, which],
            recv_sem=recv_sem.at[way, step, which],
            device_id=(s + 1 if way == 0 else s - 1, p),
            device_id_type=MESH,
        )

    def send(way, step, which, act):
        if step >= reach[which]:
            return
        slab = s - step if way == 0 else s + step
        ok = valid(-step) & valid(1) if way == 0 else valid(step) & valid(-1)

        @pl.when(ok)
        def _():
            act(copy(way, step, which, slab))

    def start(c):
        c.start()

    def take(e, which):
        if abs(e) > reach[which]:
            return
        way, step = (0 if e < 0 else 1), abs(e) - 1

        @pl.when(valid(e))
        def _():
            copy(way, step, which, s + e).wait_recv()

        send(way, step + 1, which, start)

    for which in range(4):
        for way in range(2):
            send(way, 0, which, start)

    lane = lax.broadcasted_iota(jnp.int32, (tile, pair), 1) // tile
    lane_f = lane.astype(F32)

    def basis(e):
        @pl.when(valid(e))
        def _():
            u = s + e
            ids = cg[u, blocks * slots :, :].astype(F32)
            for b in range(blocks):
                x = tg[u, b * tile : (b + 1) * tile, :].astype(F32)
                turned = pltpu.roll(x, tile, 1)
                two_t = jnp.where(lane == 0, turned, x)
                one_t = jnp.where(lane == 0, x, turned)
                g1 = ids[b : b + 1, :]
                for q in range(w // pair):
                    ts[u, b * tile : (b + 1) * tile, q * pair : (q + 1) * pair] = jnp.where(
                        lane_f + 2.0 * q == g1, one_t, 0.0
                    ).astype(BF16)
                g2 = ids[blocks + b : blocks + b + 1, :]
                for q in range(gw // pair):
                    t2s[u, b * tile : (b + 1) * tile, q * pair : (q + 1) * pair] = jnp.where(
                        lane_f + 2.0 * q == g2, two_t, 0.0
                    ).astype(BF16)

    def build(e):
        @pl.when(valid(e))
        def _():
            u = s + e
            codes = cg[u, 0 : blocks * slots, :].astype(F32)
            at = lax.broadcasted_iota(jnp.int32, (blocks * slots, pair), 1) // tile
            at = at.astype(F32)
            for cp in range(3 * rows // pair):
                hit = jnp.where(codes == at + 2.0 * cp, 1.0, 0.0)
                hot[:, :, cp * pair : (cp + 1) * pair] = hit.reshape(blocks, slots, pair)

            def row(i, carry):
                base = pl.multiple_of(i * tile, tile)
                tiles = []
                for k2 in range(slots // 2):
                    x = ag[u, pl.ds(base, tile), k2 * pair : (k2 + 1) * pair].astype(F32)
                    turned = pltpu.roll(x, tile, 1)
                    for y in (jnp.where(lane == 0, x, turned), jnp.where(lane == 0, turned, x)):
                        tiles.append(y.astype(BF16).reshape(tile // 16, 16, pair))
                for cp in range(3 * rows // pair):
                    total = None
                    for k in range(slots):
                        m = hot[i, k : k + 1, cp * pair : (cp + 1) * pair]
                        m = jnp.broadcast_to(m, (16, pair)).astype(BF16)
                        y = tiles[k] * m[None]
                        total = y if total is None else total + y
                    ad[e + 2, pl.ds(base, tile), cp * pair : (cp + 1) * pair] = total.reshape(tile, pair)
                return carry

            lax.fori_loop(0, blocks, row, 0)
            for h in range(2):
                for b in range(half):
                    x = dg[u, b * tile : (b + 1) * tile, :].astype(F32)
                    if b % 2 != h:
                        x = pltpu.roll(x, tile, 1)
                    bd[b * tile : (b + 1) * tile, (b // 2) * pair : (b // 2 + 1) * pair] = (
                        jnp.where(lane == b % 2, x, 0.0).astype(BF16)
                    )
                lo = h * half * tile
                hi = lo + half * tile
                sd[lo:hi, :] = (DAMPING * mm(bd[...], ad[e + 2, lo:hi, :])).astype(BF16)

        @pl.when(jnp.logical_not(valid(e)))
        def _():
            ad[e + 2] = jnp.zeros((rows, 3 * rows), BF16)

    def prolong(e):
        for j in range(3):
            ok = valid(e) & valid(e + j - 1)

            @pl.when(ok)
            def _(j=j):
                v = s + e + j - 1
                value = -mm(sd[:, j * rows : (j + 1) * rows], ts[v])
                if j == 1:
                    value = value + ts[v].astype(F32)
                pro[e + 2, :, j * w : (j + 1) * w] = value.astype(BF16)

            @pl.when(jnp.logical_not(ok))
            def _(j=j):
                pro[e + 2, :, j * w : (j + 1) * w] = jnp.zeros((rows, w), BF16)

    def pair_copy(m):
        return pltpu.make_async_remote_copy(
            src_ref=term.at[m, 1 - odd],
            dst_ref=rx1.at[m],
            send_sem=send1.at[m],
            recv_sem=recv1.at[m],
            device_id=(s, sibling),
            device_id_type=MESH,
        )

    def chip_copy(m, o):
        return pltpu.make_async_remote_copy(
            src_ref=tx2.at[m, o - 1],
            dst_ref=rx2.at[m, o - 1],
            send_sem=send2.at[m, o - 1],
            recv_sem=recv2.at[m, o - 1],
            device_id=(s, mates[o - 1]),
            device_id_type=MESH,
        )

    def leave(f):
        return pltpu.make_async_copy(
            cf.at[f + 3], out.at[:, pl.ds((f + 3) * w, w)], out_sem.at[f + 3]
        )

    def coarse(f):
        m = f + 3

        @pl.when(valid(f))
        def _():
            total = None
            for e in range(max(-2, f - 1), min(2, f + 1) + 1):
                j = f - e + 1
                part = mm(wm[e + 2], pro[e + 2, :, j * w : (j + 1) * w])
                total = part if total is None else total + part
            cf[m] = total
            leave(f).start()
            left = mm(t2t[...], total.astype(BF16)).astype(BF16)
            both = mm(left, t2s[s + f]).astype(BF16)
            for g in range(groups):
                term[m, g % 2, g // 2] = both[g * tile : (g + 1) * tile, :]
            pair_copy(m).start()

    def pair_sum(f):
        m = f + 3

        @pl.when(valid(f))
        def _():
            pair_copy(m).wait_recv()
            for o in range(1, chips):
                h = lax.rem(chip + o, chips)
                tx2[m, o - 1] = (term[m, odd, h].astype(F32) + rx1[m, h].astype(F32)).astype(BF16)
                chip_copy(m, o).start()
            mine[m] = term[m, odd, chip].astype(F32) + rx1[m, chip].astype(F32)

    bd[...] = jnp.zeros_like(bd)
    for f in range(-3, 4):

        @pl.when(jnp.logical_not(valid(f)))
        def _(f=f):
            cf[f + 3] = jnp.zeros((w, w), F32)
            leave(f).start()
            two[:, (f + 3) * gw : (f + 4) * gw] = jnp.zeros((tile, gw), F32)

    basis(0)
    t2t[...] = t2s[s].astype(F32).T.astype(BF16)
    build(0)
    for e in (-1, 1):
        take(e, 0)
        take(e, 1)
        basis(e)
    prolong(0)
    for e in (-1, 1):
        take(e, 2)
        take(e, 3)
    for e in (-2, 2):
        take(e, 0)
        take(e, 1)
        basis(e)
    for e in (-1, 1):
        build(e)
        prolong(e)
    turned = [
        pro[dj + 2, :, (1 - dj) * w : (2 - dj) * w].astype(F32).T.astype(BF16) for dj in (-1, 0, 1)
    ]
    for e in range(-2, 3):
        total = None
        for dj in (-1, 0, 1):
            j = e - dj + 1
            if 0 <= j < 3:
                part = mm(turned[dj + 1], ad[dj + 2, :, j * rows : (j + 1) * rows])
                total = part if total is None else total + part
        wm[e + 2] = total.astype(BF16)
    coarse(0)
    for e in (-3, 3):
        take(e, 0)
        take(e, 1)
        basis(e)
    order = [0]
    for way in (-1, 1):
        take(2 * way, 2)
        take(2 * way, 3)
        build(2 * way)
        prolong(2 * way)
        for f in (way, 2 * way, 3 * way):
            coarse(f)
            pair_sum(order[-1])
            order.append(f)
    pair_sum(order[-1])
    for f in order:
        m = f + 3

        @pl.when(valid(f))
        def _(m=m):
            total = mine[m]
            for o in range(1, chips):
                chip_copy(m, o).wait_recv()
                total = total + rx2[m, o - 1].astype(F32)
            two[:, m * gw : (m + 1) * gw] = total

    for f in range(-3, 4):
        m = f + 3
        leave(f).wait()

        @pl.when(valid(f))
        def _(m=m):
            pair_copy(m).wait_send()
            for o in range(1, chips):
                chip_copy(m, o).wait_send()

    for step in range(far):
        for which in range(4):
            for way in range(2):
                send(way, step, which, lambda c: c.wait_send())


def at_once(
    fine_tiles, fine_cols, bond_mask, diag_inv, tentative, aggregate, tentative_two, aggregate_two
):
    blocks, tile = diag_inv.shape[0], diag_inv.shape[1]
    slots = fine_cols.shape[1]
    aggs = tentative_two.shape[0]
    n, groups = lax.axis_size("slab"), lax.axis_size("piece")
    rows, w, gw = blocks * tile, aggs * tile, groups * tile
    pair, chips, far = 2 * tile, groups // 2, min(3, n - 1)
    codes = jnp.concatenate(
        [jnp.where(bond_mask != 0, fine_cols, -1).reshape(-1), aggregate, aggregate_two]
    )
    codes = jnp.broadcast_to(codes.astype(BF16)[:, None], (codes.shape[0], pair))
    vmem = pl.BlockSpec(memory_space=pltpu.VMEM)
    dma = pltpu.SemaphoreType.DMA
    scratch = [
        pltpu.VMEM((n, rows, slots * tile), BF16),
        pltpu.VMEM((n, rows // 2, pair), BF16),
        pltpu.VMEM((n, rows, pair), BF16),
        pltpu.VMEM((n, codes.shape[0], pair), BF16),
        pltpu.VMEM((5, rows, 3 * rows), BF16),
        pltpu.VMEM((rows, 3 * rows), BF16),
        pltpu.VMEM((5, rows, 3 * w), BF16),
        pltpu.VMEM((n, rows, w), BF16),
        pltpu.VMEM((n, w, gw), BF16),
        pltpu.VMEM((gw, w), BF16),
        pltpu.VMEM((blocks, slots, 3 * rows), F32),
        pltpu.VMEM((rows // 2, rows // 2), BF16),
        pltpu.VMEM((5, w, rows), BF16),
        pltpu.VMEM((7, w, w), F32),
        pltpu.VMEM((7, 2, chips, tile, gw), BF16),
        pltpu.VMEM((7, tile, gw), F32),
        pltpu.VMEM((7, chips, tile, gw), BF16),
        pltpu.VMEM((7, chips - 1, tile, gw), BF16),
        pltpu.VMEM((7, chips - 1, tile, gw), BF16),
    ]
    size = sum(x.dtype.itemsize * np.prod(x.shape) for x in scratch)
    if size > FUSED_LIMIT:
        return None
    coarse, level_two = pl.pallas_call(
        functools.partial(whole_kernel, n, blocks, slots, aggs, groups, tile),
        out_shape=(
            jax.ShapeDtypeStruct((w, 7 * w), F32),
            jax.ShapeDtypeStruct((tile, 7 * gw), F32),
        ),
        in_specs=[vmem] * 5,
        out_specs=(pl.BlockSpec(memory_space=pl.ANY), vmem),
        scratch_shapes=scratch
        + [
            dma((2, far, 4)),
            dma((2, far, 4)),
            dma((7,)),
            dma((7,)),
            dma((7,)),
            dma((7, chips - 1)),
            dma((7, chips - 1)),
        ],
        compiler_params=pltpu.CompilerParams(
            collective_id=2, has_side_effects=True, vmem_limit_bytes=VMEM_LIMIT
        ),
    )(
        fine_tiles.reshape(rows, slots * tile),
        diag_inv.reshape(rows, tile),
        tentative.reshape(rows, tile),
        tentative_two.reshape(w, tile),
        codes,
    )
    return (coarse.reshape(aggs, tile, 7 * w), level_two.reshape(1, tile, 7 * gw))


def per_device(*args):
    done = at_once(*args)
    return in_stages(*args) if done is None else done


def solution(mesh):
    placed = (
        P(("slab", "piece"), None, None),
        P(("slab", "piece"), None),
        P(("slab", "piece"), None),
        P(("slab", "piece"), None, None),
        P(("slab", "piece"), None, None),
        P(("slab", "piece")),
        P(("slab", "piece"), None, None),
        P(("slab", "piece")),
    )
    return jax.shard_map(
        per_device,
        mesh=mesh,
        in_specs=placed,
        out_specs=(P(("slab", "piece"), None, None), P(("slab", "piece"), None, None)),
        check_vma=False,
    )
```

```python
import functools

import jax
import jax.numpy as jnp
import numpy as np
from jax import lax
from jax.experimental import pallas as pl
from jax.experimental.pallas import tpu as pltpu
from jax.sharding import PartitionSpec as P

DAMPING = 2.0 / 3.0
LANES = 128
MESH = pl.DeviceIdType.MESH
VMEM_LIMIT = 60 * 1024 * 1024
FUSED_LIMIT = 50 * 1024 * 1024
F32 = jnp.float32
BF16 = jnp.bfloat16


def mm(a, b):
    return jnp.dot(a, b, preferred_element_type=F32)


def gather_kernel(n, far, a_ref, d_ref, t_ref, q_ref, i_ref, ag, dg, tg, ig, send_sem, recv_sem):
    s, p = lax.axis_index("slab"), lax.axis_index("piece")
    barrier = pltpu.get_barrier_semaphore()

    @pl.when(s > 0)
    def _():
        pl.semaphore_signal(barrier, inc=1, device_id=(s - 1, p), device_id_type=MESH)

    @pl.when(s < n - 1)
    def _():
        pl.semaphore_signal(barrier, inc=1, device_id=(s + 1, p), device_id_type=MESH)

    half = d_ref.shape[0] // 2
    ag[s] = a_ref[...]
    dg[s] = jnp.concatenate([d_ref[0:half, :], d_ref[half : 2 * half, :]], axis=1)
    tg[s] = jnp.concatenate([t_ref[...], q_ref[...]], axis=1)
    ig[s] = i_ref[...]

    peers = jnp.where(s > 0, 1, 0) + jnp.where(s < n - 1, 1, 0)
    pl.semaphore_wait(barrier, peers)

    arrays = (ig, tg, dg, ag)
    reach = (far, far, 2, 2)

    def copy(way, step, which, slab):
        there = s + 1 if way == 0 else s - 1
        return pltpu.make_async_remote_copy(
            src_ref=arrays[which].at[slab],
            dst_ref=arrays[which].at[slab],
            send_sem=send_sem.at[way, step, which],
            recv_sem=recv_sem.at[way, step, which],
            device_id=(there, p),
            device_id_type=MESH,
        )

    def sends(way, step):
        if way == 0:
            return (s - step >= 0) & (s + 1 < n), s - step
        return (s + step < n) & (s >= 1), s + step

    def gets(way, step):
        if way == 0:
            return s - 1 - step >= 0, s - 1 - step
        return s + 1 + step < n, s + 1 + step

    steps = min(far, n - 1)
    for step in range(steps + 1):
        for which in range(4):
            for way in range(2):
                if 0 < step <= min(reach[which], steps):
                    ok, slab = gets(way, step - 1)

                    @pl.when(ok)
                    def _(way=way, which=which, slab=slab):
                        copy(way, step - 1, which, slab).wait_recv()

                if step < min(reach[which], steps):
                    ok, slab = sends(way, step)

                    @pl.when(ok)
                    def _(way=way, which=which, slab=slab):
                        copy(way, step, which, slab).start()

    for step in range(steps):
        for which in range(4):
            for way in range(2):
                if step < reach[which]:
                    ok, slab = sends(way, step)

                    @pl.when(ok)
                    def _(way=way, which=which, slab=slab):
                        copy(way, step, which, slab).wait_send()


def level_kernel(
    n, blocks, slots, aggs, groups, tile, s_ref, i_ref, ag, dg, tg,
    out, cb, t2s, t2t, ad, sd, pro, ts, acc, bd, wm,
):
    s = s_ref[0]
    rows, w, gw = blocks * tile, aggs * tile, groups * tile
    pair = 2 * tile
    lane = lax.broadcasted_iota(jnp.int32, (tile, pair), 1) // tile

    for v in range(n):
        near = jnp.abs(v - s) <= 3
        for b in range(blocks):
            x = tg[v, b * tile : (b + 1) * tile, :].astype(F32)
            turned = pltpu.roll(x, tile, 1)
            one = jnp.where(lane == 0, x, turned)
            two = jnp.where(lane == 0, turned, x)
            g1 = jnp.where(near, i_ref[v, 2, b], -1)
            g2 = jnp.where(near, i_ref[v, 3, b], -1)
            for q in range(w // pair):
                ts[v, b * tile : (b + 1) * tile, q * pair : (q + 1) * pair] = jnp.where(
                    lane + 2 * q == g1, one, 0.0
                ).astype(BF16)
            for q in range(gw // pair):
                t2s[v, b * tile : (b + 1) * tile, q * pair : (q + 1) * pair] = jnp.where(
                    lane + 2 * q == g2, two, 0.0
                ).astype(BF16)

    t2t[...] = t2s[s].astype(F32).T.astype(BF16)
    bd[...] = jnp.zeros_like(bd)

    for e in range(-2, 3):
        u = s + e

        @pl.when((u >= 0) & (u < n))
        def _(e=e, u=u):
            def row(i, carry):
                acc[...] = jnp.zeros_like(acc)
                base = pl.multiple_of(i * tile, tile)
                for k2 in range(slots // 2):
                    x = ag[u, pl.ds(base, tile), k2 * pair : (k2 + 1) * pair].astype(F32)
                    turned = pltpu.roll(x, tile, 1)
                    for odd in range(2):
                        k = 2 * k2 + odd
                        c = i_ref[u, 0, i * slots + k]
                        m = i_ref[u, 1, i * slots + k]
                        side = lax.rem(c, 2)
                        y = jnp.where(side == odd, x, turned)
                        keep = jnp.where(m != 0, side, -1)
                        at = pl.multiple_of((c // 2) * pair, pair)
                        acc[:, pl.ds(at, pair)] += jnp.where(lane == keep, y, 0.0)
                ad[e + 2, pl.ds(base, tile), :] = acc[...].astype(BF16)
                return carry

            lax.fori_loop(0, blocks, row, 0)
            half = blocks // 2
            for h in range(2):
                for b in range(half):
                    x = dg[u, b * tile : (b + 1) * tile, :].astype(F32)
                    if b % 2 != h:
                        x = pltpu.roll(x, tile, 1)
                    bd[b * tile : (b + 1) * tile, (b // 2) * pair : (b // 2 + 1) * pair] = (
                        jnp.where(lane == b % 2, x, 0.0).astype(BF16)
                    )
                lo = h * half * tile
                hi = lo + half * tile
                sd[lo:hi, :] = (DAMPING * mm(bd[...], ad[e + 2, lo:hi, :])).astype(BF16)
            for j in range(3):
                v = u + j - 1
                inside = (v >= 0) & (v < n)

                @pl.when(inside)
                def _(j=j, v=v):
                    value = -mm(sd[:, j * rows : (j + 1) * rows], ts[v])
                    if j == 1:
                        value = value + ts[v].astype(F32)
                    pro[e + 2, :, j * w : (j + 1) * w] = value.astype(BF16)

                @pl.when(jnp.logical_not(inside))
                def _(j=j):
                    pro[e + 2, :, j * w : (j + 1) * w] = jnp.zeros((rows, w), BF16)

        @pl.when((u < 0) | (u >= n))
        def _(e=e):
            pro[e + 2] = jnp.zeros((rows, 3 * w), BF16)
            if abs(e) < 2:
                ad[e + 2] = jnp.zeros((rows, 3 * rows), BF16)

    turned = [pro[dj + 2, :, (1 - dj) * w : (2 - dj) * w].astype(F32).T.astype(BF16) for dj in (-1, 0, 1)]
    for e in range(-2, 3):
        total = None
        for dj in (-1, 0, 1):
            j = e - dj + 1
            if 0 <= j < 3:
                term = mm(turned[dj + 1], ad[dj + 2, :, j * rows : (j + 1) * rows])
                total = term if total is None else total + term
        wm[e + 2] = total.astype(BF16)

    short = n < 7
    for f in range(-3, 4):
        t = s + f
        inside = (t >= 0) & (t < n)

        @pl.when(inside)
        def _(f=f, t=t):
            total = None
            for e in range(max(-2, f - 1), min(2, f + 1) + 1):
                j = f - e + 1
                term = mm(wm[e + 2], pro[e + 2, :, j * w : (j + 1) * w])
                total = term if total is None else total + term
            out[:, (f + 3) * w : (f + 4) * w] = total
            cb[t if short else f + 3] = total.astype(BF16)

        @pl.when(jnp.logical_not(inside))
        def _(f=f):
            out[:, (f + 3) * w : (f + 4) * w] = jnp.zeros((w, w), F32)
            if not short:
                cb[f + 3] = jnp.zeros((w, w), BF16)


def scatter_kernel(
    n, parts, groups, tile, cb, t2s, t2t, out, term, mine, rx1, tx2, rx2,
    send1, recv1, send2, recv2,
):
    s, p = lax.axis_index("slab"), lax.axis_index("piece")
    chips = groups // 2
    odd = lax.rem(p, 2)
    chip = p // 2
    sibling = p + 1 - 2 * odd
    gw = groups * tile
    mates = [2 * lax.rem(chip + o, chips) + odd for o in range(1, chips)]

    barrier = pltpu.get_barrier_semaphore()
    for mate in [sibling] + mates:
        pl.semaphore_signal(barrier, inc=1, device_id=(s, mate), device_id_type=MESH)
    if n < 7:
        out[...] = jnp.zeros_like(out)
    pl.semaphore_wait(barrier, chips)

    def pair_copy(m):
        return pltpu.make_async_remote_copy(
            src_ref=term.at[m, 1 - odd],
            dst_ref=rx1.at[m],
            send_sem=send1.at[m],
            recv_sem=recv1.at[m],
            device_id=(s, sibling),
            device_id_type=MESH,
        )

    def chip_copy(m, o):
        return pltpu.make_async_remote_copy(
            src_ref=tx2.at[m, o - 1],
            dst_ref=rx2.at[m, o - 1],
            send_sem=send2.at[m, o - 1],
            recv_sem=recv2.at[m, o - 1],
            device_id=(s, mates[o - 1]),
            device_id_type=MESH,
        )

    def pair_sum(m):
        pair_copy(m).wait_recv()
        for o in range(1, chips):
            h = lax.rem(chip + o, chips)
            tx2[m, o - 1] = (term[m, odd, h].astype(F32) + rx1[m, h].astype(F32)).astype(BF16)
            chip_copy(m, o).start()
        mine[m] = term[m, odd, chip].astype(F32) + rx1[m, chip].astype(F32)

    for m in range(parts):
        v = m if n < 7 else jnp.clip(s + m - 3, 0, n - 1)
        left = mm(t2t[...], cb[m]).astype(BF16)
        both = mm(left, t2s[v]).astype(BF16)
        for g in range(groups):
            term[m, g % 2, g // 2] = both[g * tile : (g + 1) * tile, :]
        pair_copy(m).start()
        if m > 0:
            pair_sum(m - 1)
    pair_sum(parts - 1)
    for m in range(parts):
        total = mine[m]
        for o in range(1, chips):
            chip_copy(m, o).wait_recv()
            total = total + rx2[m, o - 1].astype(F32)
        place = (m + 3 - s) * gw if n < 7 else m * gw
        out[:, pl.ds(pl.multiple_of(place, LANES), gw)] = total
    for m in range(parts):
        pair_copy(m).wait_send()
        for o in range(1, chips):
            chip_copy(m, o).wait_send()


def in_stages(
    fine_tiles, fine_cols, bond_mask, diag_inv, tentative, aggregate, tentative_two, aggregate_two
):
    blocks, tile = diag_inv.shape[0], diag_inv.shape[1]
    slots = fine_cols.shape[1]
    aggs = tentative_two.shape[0]
    n, groups = lax.axis_size("slab"), lax.axis_size("piece")
    rows, w, gw = blocks * tile, aggs * tile, groups * tile
    parts = min(7, n)
    vmem = pl.BlockSpec(memory_space=pltpu.VMEM)
    smem = pl.BlockSpec(memory_space=pltpu.SMEM)
    shape = jax.ShapeDtypeStruct

    width = -(-blocks * slots // LANES) * LANES

    def line(x):
        x = x.reshape(1, -1)
        return jnp.pad(x, ((0, 0), (0, width - x.shape[1])))

    ints = jnp.concatenate([line(fine_cols), line(bond_mask), line(aggregate), line(aggregate_two)], 0)
    ints = jnp.pad(ints, ((0, 4), (0, 0)))

    far = min(3, n - 1)
    ag, dg, tg, ig = pl.pallas_call(
        functools.partial(gather_kernel, n, far),
        out_shape=(
            shape((n, rows, slots * tile), BF16),
            shape((n, rows // 2, 2 * tile), BF16),
            shape((n, rows, 2 * tile), BF16),
            shape((n, 8, width), jnp.int32),
        ),
        in_specs=[vmem] * 5,
        out_specs=(vmem,) * 4,
        scratch_shapes=[
            pltpu.SemaphoreType.DMA((2, far, 4)),
            pltpu.SemaphoreType.DMA((2, far, 4)),
        ],
        compiler_params=pltpu.CompilerParams(
            collective_id=0, has_side_effects=True, vmem_limit_bytes=VMEM_LIMIT
        ),
    )(
        fine_tiles.reshape(rows, slots * tile),
        diag_inv.reshape(rows, tile),
        tentative.reshape(rows, tile),
        tentative_two.reshape(w, tile),
        ints,
    )

    slab = lax.axis_index("slab").astype(jnp.int32).reshape(1)
    coarse, cb, t2s, t2t = pl.pallas_call(
        functools.partial(level_kernel, n, blocks, slots, aggs, groups, tile),
        out_shape=(
            shape((w, 7 * w), F32),
            shape((parts, w, w), BF16),
            shape((n, w, gw), BF16),
            shape((gw, w), BF16),
        ),
        in_specs=[smem, smem, vmem, vmem, vmem],
        out_specs=(vmem,) * 4,
        scratch_shapes=[
            pltpu.VMEM((5, rows, 3 * rows), BF16),
            pltpu.VMEM((rows, 3 * rows), BF16),
            pltpu.VMEM((5, rows, 3 * w), BF16),
            pltpu.VMEM((n, rows, w), BF16),
            pltpu.VMEM((tile, 3 * rows), F32),
            pltpu.VMEM((rows // 2, rows // 2), BF16),
            pltpu.VMEM((5, w, rows), BF16),
        ],
        compiler_params=pltpu.CompilerParams(vmem_limit_bytes=VMEM_LIMIT),
    )(slab, ig, ag, dg, tg)

    chips = groups // 2
    level_two = pl.pallas_call(
        functools.partial(scatter_kernel, n, parts, groups, tile),
        out_shape=shape((tile, 7 * gw), F32),
        in_specs=[vmem] * 3,
        out_specs=vmem,
        scratch_shapes=[
            pltpu.VMEM((parts, 2, chips, tile, gw), BF16),
            pltpu.VMEM((parts, tile, gw), F32),
            pltpu.VMEM((parts, chips, tile, gw), BF16),
            pltpu.VMEM((parts, chips - 1, tile, gw), BF16),
            pltpu.VMEM((parts, chips - 1, tile, gw), BF16),
            pltpu.SemaphoreType.DMA((parts,)),
            pltpu.SemaphoreType.DMA((parts,)),
            pltpu.SemaphoreType.DMA((parts, chips - 1)),
            pltpu.SemaphoreType.DMA((parts, chips - 1)),
        ],
        compiler_params=pltpu.CompilerParams(
            collective_id=1, has_side_effects=True, vmem_limit_bytes=VMEM_LIMIT
        ),
    )(cb, t2s, t2t)

    return (coarse.reshape(aggs, tile, 7 * w), level_two.reshape(1, tile, 7 * gw))


def whole_kernel(
    n, blocks, slots, aggs, groups, tile,
    a_ref, d_ref, t_ref, q_ref, cols_ref, mask_ref, one_ref, two_ref, out, two,
    ag, dg, tg, cg, ad, sd, pro, ts, t2s, t2t, hot, ids, bd, wm, cf, term, mine, rx1, tx2, rx2,
    send_sem, recv_sem, out_sem, send1, recv1, send2, recv2,
):
    s, p = lax.axis_index("slab"), lax.axis_index("piece")
    far = min(3, n - 1)
    rows, w, gw = blocks * tile, aggs * tile, groups * tile
    pair, half = 2 * tile, blocks // 2
    chips = groups // 2
    odd, chip = lax.rem(p, 2), p // 2
    sibling = p + 1 - 2 * odd
    mates = [2 * lax.rem(chip + o, chips) + odd for o in range(1, chips)]
    barrier = pltpu.get_barrier_semaphore()

    @pl.when(s > 0)
    def _():
        pl.semaphore_signal(barrier, inc=1, device_id=(s - 1, p), device_id_type=MESH)

    @pl.when(s < n - 1)
    def _():
        pl.semaphore_signal(barrier, inc=1, device_id=(s + 1, p), device_id_type=MESH)

    for mate in [sibling] + mates:
        pl.semaphore_signal(barrier, inc=1, device_id=(s, mate), device_id_type=MESH)

    for i in range(blocks):
        for k in range(slots):
            code = jnp.where(mask_ref[i, k] != 0, cols_ref[i, k], -1)
            ids[i * slots + k : i * slots + k + 1, :] = jnp.full((1, pair), code, jnp.int32)
        at = blocks * slots + i
        ids[at : at + 1, :] = jnp.full((1, pair), one_ref[i], jnp.int32)
        ids[at + blocks : at + blocks + 1, :] = jnp.full((1, pair), two_ref[i], jnp.int32)
    cg[s] = ids[...].astype(F32).astype(BF16)
    tg[s] = jnp.concatenate([t_ref[...], q_ref[...]], axis=1)
    dg[s] = jnp.concatenate([d_ref[0 : rows // 2, :], d_ref[rows // 2 : rows, :]], axis=1)
    ag[s] = a_ref[...]
    peers = chips + jnp.where(s > 0, 1, 0) + jnp.where(s < n - 1, 1, 0)
    pl.semaphore_wait(barrier, peers)

    kinds = 5
    reach = (far, far) + (min(2, far),) * 3

    def part_of(which, slab):
        if which < 3:
            return (cg, tg, dg)[which].at[slab]
        return ag.at[slab, pl.ds((which - 3) * (rows // 2), rows // 2)]

    def valid(e):
        return (s + e >= 0) & (s + e < n)

    def copy(way, step, which, slab):
        return pltpu.make_async_remote_copy(
            src_ref=part_of(which, slab),
            dst_ref=part_of(which, slab),
            send_sem=send_sem.at[way, step, which],
            recv_sem=recv_sem.at[way, step, which],
            device_id=(s + 1 if way == 0 else s - 1, p),
            device_id_type=MESH,
        )

    def send(way, step, which, act):
        if step >= reach[which]:
            return
        slab = s - step if way == 0 else s + step
        ok = valid(-step) & valid(1) if way == 0 else valid(step) & valid(-1)

        @pl.when(ok)
        def _():
            act(copy(way, step, which, slab))

    def start(c):
        c.start()

    def take(e, which):
        if abs(e) > reach[which]:
            return
        way, step = (0 if e < 0 else 1), abs(e) - 1

        @pl.when(valid(e))
        def _():
            copy(way, step, which, s + e).wait_recv()

        send(way, step + 1, which, start)

    for which in range(kinds):
        for way in range(2):
            send(way, 0, which, start)

    lane = lax.broadcasted_iota(jnp.int32, (tile, pair), 1) // tile
    lane_f = lane.astype(F32)

    def basis(e):
        @pl.when(valid(e))
        def _():
            u = s + e
            names = cg[u, blocks * slots :, :].astype(F32)
            for b in range(blocks):
                x = tg[u, b * tile : (b + 1) * tile, :].astype(F32)
                turned = pltpu.roll(x, tile, 1)
                two_t = jnp.where(lane == 0, turned, x)
                one_t = jnp.where(lane == 0, x, turned)
                g1 = names[b : b + 1, :]
                for q in range(w // pair):
                    ts[u, b * tile : (b + 1) * tile, q * pair : (q + 1) * pair] = jnp.where(
                        lane_f + 2.0 * q == g1, one_t, 0.0
                    ).astype(BF16)
                g2 = names[blocks + b : blocks + b + 1, :]
                for q in range(gw // pair):
                    t2s[u, b * tile : (b + 1) * tile, q * pair : (q + 1) * pair] = jnp.where(
                        lane_f + 2.0 * q == g2, two_t, 0.0
                    ).astype(BF16)

    def build(e, h):
        lo, hi = h * half * tile, (h + 1) * half * tile

        @pl.when(valid(e))
        def _():
            u = s + e
            if h == 0:
                codes = cg[u, 0 : blocks * slots, :].astype(F32)
                at = lax.broadcasted_iota(jnp.int32, (blocks * slots, pair), 1) // tile
                at = at.astype(F32)
                for cp in range(3 * rows // pair):
                    hit = jnp.where(codes == at + 2.0 * cp, 1.0, 0.0)
                    hot[:, :, cp * pair : (cp + 1) * pair] = hit.reshape(blocks, slots, pair)

            def row(i, carry):
                base = pl.multiple_of(i * tile, tile)
                tiles = []
                for k2 in range(slots // 2):
                    x = ag[u, pl.ds(base, tile), k2 * pair : (k2 + 1) * pair].astype(F32)
                    turned = pltpu.roll(x, tile, 1)
                    for y in (jnp.where(lane == 0, x, turned), jnp.where(lane == 0, turned, x)):
                        tiles.append(y.astype(BF16).reshape(tile // 16, 16, pair))
                for cp in range(3 * rows // pair):
                    total = None
                    for k in range(slots):
                        m = hot[i, k : k + 1, cp * pair : (cp + 1) * pair]
                        m = jnp.broadcast_to(m, (16, pair)).astype(BF16)
                        y = tiles[k] * m[None]
                        total = y if total is None else total + y
                    ad[e + 2, pl.ds(base, tile), cp * pair : (cp + 1) * pair] = total.reshape(tile, pair)
                return carry

            lax.fori_loop(h * half, (h + 1) * half, row, 0)
            for b in range(half):
                x = dg[u, b * tile : (b + 1) * tile, :].astype(F32)
                if b % 2 != h:
                    x = pltpu.roll(x, tile, 1)
                bd[b * tile : (b + 1) * tile, (b // 2) * pair : (b // 2 + 1) * pair] = (
                    jnp.where(lane == b % 2, x, 0.0).astype(BF16)
                )
            sd[lo:hi, :] = (DAMPING * mm(bd[...], ad[e + 2, lo:hi, :])).astype(BF16)

        if abs(e) < 2:

            @pl.when(jnp.logical_not(valid(e)))
            def _():
                ad[e + 2, lo:hi, :] = jnp.zeros((hi - lo, 3 * rows), BF16)

    def prolong(e, j, lo, hi):
        ok = valid(e) & valid(e + j - 1)

        @pl.when(ok)
        def _():
            v = s + e + j - 1
            value = -mm(sd[lo:hi, j * rows : (j + 1) * rows], ts[v])
            if j == 1:
                value = value + ts[v, lo:hi, :].astype(F32)
            pro[e + 2, lo:hi, j * w : (j + 1) * w] = value.astype(BF16)

        @pl.when(jnp.logical_not(ok))
        def _():
            pro[e + 2, lo:hi, j * w : (j + 1) * w] = jnp.zeros((hi - lo, w), BF16)

    def pair_copy(m):
        return pltpu.make_async_remote_copy(
            src_ref=term.at[m, 1 - odd],
            dst_ref=rx1.at[m],
            send_sem=send1.at[m],
            recv_sem=recv1.at[m],
            device_id=(s, sibling),
            device_id_type=MESH,
        )

    def chip_copy(m, o):
        return pltpu.make_async_remote_copy(
            src_ref=tx2.at[m, o - 1],
            dst_ref=rx2.at[m, o - 1],
            send_sem=send2.at[m, o - 1],
            recv_sem=recv2.at[m, o - 1],
            device_id=(s, mates[o - 1]),
            device_id_type=MESH,
        )

    def leave(f):
        return pltpu.make_async_copy(
            cf.at[f + 3], out.at[f + 3], out_sem.at[f + 3]
        )

    def sum_over(f, sides):
        total = None
        for e in sides:
            j = f - e + 1
            part = mm(wm[e + 2], pro[e + 2, :, j * w : (j + 1) * w])
            total = part if total is None else total + part
        return total

    def early(f):
        sides = [e for e in (-1, 0, 1) if abs(f - e) < 2]

        @pl.when(valid(f))
        def _():
            cf[f + 3] = sum_over(f, sides)

    def coarse(f):
        m = f + 3

        @pl.when(valid(f))
        def _():
            if abs(f) == 3:
                cf[m] = sum_over(f, [2 if f > 0 else -2])
            elif f != 0:
                cf[m] += sum_over(f, [2 if f > 0 else -2])
            leave(f).start()
            left = mm(t2t[...], cf[m].astype(BF16)).astype(BF16)
            both = mm(left, t2s[s + f]).astype(BF16)
            for g in range(groups):
                term[m, g % 2, g // 2] = both[g * tile : (g + 1) * tile, :]
            pair_copy(m).start()

    def pair_sum(f):
        m = f + 3

        @pl.when(valid(f))
        def _():
            pair_copy(m).wait_recv()
            for o in range(1, chips):
                h = lax.rem(chip + o, chips)
                tx2[m, o - 1] = (term[m, odd, h].astype(F32) + rx1[m, h].astype(F32)).astype(BF16)
                chip_copy(m, o).start()
            mine[m] = term[m, odd, chip].astype(F32) + rx1[m, chip].astype(F32)

    bd[...] = jnp.zeros_like(bd)
    for f in range(-3, 4):

        @pl.when(jnp.logical_not(valid(f)))
        def _(f=f):
            two[:, (f + 3) * gw : (f + 4) * gw] = jnp.zeros((tile, gw), F32)

    basis(0)
    t2t[...] = t2s[s].astype(F32).T.astype(BF16)
    build(0, 0)
    build(0, 1)
    for e in (-1, 1):
        take(e, 0)
        take(e, 1)
        basis(e)
    for j in range(3):
        prolong(0, j, 0, rows)
    for h in range(2):
        for e in (-1, 1):
            if h == 0:
                take(e, 2)
            take(e, 3 + h)
    for e in (-2, 2):
        take(e, 0)
        take(e, 1)
        basis(e)
    for e in (-1, 1):
        build(e, 0)
        build(e, 1)
        for j in range(3):
            prolong(e, j, 0, rows)
    turned = [
        pro[dj + 2, :, (1 - dj) * w : (2 - dj) * w].astype(F32).T.astype(BF16) for dj in (-1, 0, 1)
    ]
    for e in range(-2, 3):
        total = None
        for dj in (-1, 0, 1):
            j = e - dj + 1
            if 0 <= j < 3:
                part = mm(turned[dj + 1], ad[dj + 2, :, j * rows : (j + 1) * rows])
                total = part if total is None else total + part
        wm[e + 2] = total.astype(BF16)
    early(0)
    coarse(0)
    for f in (-2, -1, 1, 2):
        early(f)
    pair_sum(0)
    for e in (-3, 3):
        take(e, 0)
        take(e, 1)
        basis(e)
    order = [0]
    for way in (-1, 1):
        e = 2 * way
        take(e, 2)
        take(e, 3)
        build(e, 0)
        for j in range(3):
            prolong(e, j, 0, rows // 2)
        take(e, 4)
        build(e, 1)
        for f in (way, 2 * way, 3 * way):
            prolong(e, f - e + 1, rows // 2, rows)
            coarse(f)
            if order[-1] != 0:
                pair_sum(order[-1])
            order.append(f)
    pair_sum(order[-1])
    for f in order:
        m = f + 3

        @pl.when(valid(f))
        def _(m=m):
            total = mine[m]
            for o in range(1, chips):
                chip_copy(m, o).wait_recv()
                total = total + rx2[m, o - 1].astype(F32)
            two[:, m * gw : (m + 1) * gw] = total

    for f in range(-3, 4):
        m = f + 3

        @pl.when(valid(f))
        def _(f=f, m=m):
            leave(f).wait()
            pair_copy(m).wait_send()
            for o in range(1, chips):
                chip_copy(m, o).wait_send()

    for step in range(far):
        for which in range(kinds):
            for way in range(2):
                send(way, step, which, lambda c: c.wait_send())


def place_kernel(n, blocks, level, out, two, held, zero, in_sem, out_sem):
    s = lax.axis_index("slab")
    w = zero.shape[0]

    def write(f, source):
        return pltpu.make_async_copy(source, out.at[:, pl.ds((f + 3) * w, w)], out_sem.at[f + 3])

    def read(f):
        return pltpu.make_async_copy(blocks.at[f + 3], held.at[f + 3], in_sem.at[f + 3])

    def either(f, inside, outside):
        ok = (s + f >= 0) & (s + f < n)

        @pl.when(ok)
        def _():
            inside()

        if outside is not None:

            @pl.when(jnp.logical_not(ok))
            def _():
                outside()

    for f in range(-3, 4):
        either(f, lambda: read(f).start(), None)
    zero[...] = jnp.zeros_like(zero)
    for f in range(-3, 4):
        either(f, lambda: None, lambda: write(f, zero).start())

    def onward(f):
        read(f).wait()
        write(f, held.at[f + 3]).start()

    for f in range(-3, 4):
        either(f, lambda: onward(f), None)
    two[...] = level[...]
    for f in range(-3, 4):
        either(f, lambda: write(f, held.at[f + 3]).wait(), lambda: write(f, zero).wait())


def at_once(
    fine_tiles, fine_cols, bond_mask, diag_inv, tentative, aggregate, tentative_two, aggregate_two
):
    blocks, tile = diag_inv.shape[0], diag_inv.shape[1]
    slots = fine_cols.shape[1]
    aggs = tentative_two.shape[0]
    n, groups = lax.axis_size("slab"), lax.axis_size("piece")
    rows, w, gw = blocks * tile, aggs * tile, groups * tile
    pair, chips, far = 2 * tile, groups // 2, min(3, n - 1)
    names = blocks * slots + 2 * blocks
    vmem = pl.BlockSpec(memory_space=pltpu.VMEM)
    smem = pl.BlockSpec(memory_space=pltpu.SMEM)
    dma = pltpu.SemaphoreType.DMA
    scratch = [
        pltpu.VMEM((n, rows, slots * tile), BF16),
        pltpu.VMEM((n, rows // 2, pair), BF16),
        pltpu.VMEM((n, rows, pair), BF16),
        pltpu.VMEM((n, names, pair), BF16),
        pltpu.VMEM((5, rows, 3 * rows), BF16),
        pltpu.VMEM((rows, 3 * rows), BF16),
        pltpu.VMEM((5, rows, 3 * w), BF16),
        pltpu.VMEM((n, rows, w), BF16),
        pltpu.VMEM((n, w, gw), BF16),
        pltpu.VMEM((gw, w), BF16),
        pltpu.VMEM((blocks, slots, 3 * rows), F32),
        pltpu.VMEM((names, pair), jnp.int32),
        pltpu.VMEM((rows // 2, rows // 2), BF16),
        pltpu.VMEM((5, w, rows), BF16),
        pltpu.VMEM((7, w, w), F32),
        pltpu.VMEM((7, 2, chips, tile, gw), BF16),
        pltpu.VMEM((7, tile, gw), F32),
        pltpu.VMEM((7, chips, tile, gw), BF16),
        pltpu.VMEM((7, chips - 1, tile, gw), BF16),
        pltpu.VMEM((7, chips - 1, tile, gw), BF16),
    ]
    size = sum(x.dtype.itemsize * np.prod(x.shape) for x in scratch)
    if size > FUSED_LIMIT:
        return None
    held, level_two = pl.pallas_call(
        functools.partial(whole_kernel, n, blocks, slots, aggs, groups, tile),
        out_shape=(
            jax.ShapeDtypeStruct((7, w, w), F32),
            jax.ShapeDtypeStruct((tile, 7 * gw), F32),
        ),
        in_specs=[vmem] * 4 + [smem] * 4,
        out_specs=(pl.BlockSpec(memory_space=pl.ANY), vmem),
        scratch_shapes=scratch
        + [
            dma((2, far, 5)),
            dma((2, far, 5)),
            dma((7,)),
            dma((7,)),
            dma((7,)),
            dma((7, chips - 1)),
            dma((7, chips - 1)),
        ],
        compiler_params=pltpu.CompilerParams(
            collective_id=2, has_side_effects=True, vmem_limit_bytes=VMEM_LIMIT
        ),
    )(
        fine_tiles.reshape(rows, slots * tile),
        diag_inv.reshape(rows, tile),
        tentative.reshape(rows, tile),
        tentative_two.reshape(w, tile),
        fine_cols,
        bond_mask,
        aggregate,
        aggregate_two,
    )
    coarse, level_two = pl.pallas_call(
        functools.partial(place_kernel, n),
        out_shape=(
            jax.ShapeDtypeStruct((w, 7 * w), F32),
            jax.ShapeDtypeStruct((tile, 7 * gw), F32),
        ),
        in_specs=[pl.BlockSpec(memory_space=pl.ANY), vmem],
        out_specs=(pl.BlockSpec(memory_space=pl.ANY), vmem),
        scratch_shapes=[
            pltpu.VMEM((7, w, w), F32),
            pltpu.VMEM((w, w), F32),
            dma((7,)),
            dma((7,)),
        ],
        compiler_params=pltpu.CompilerParams(vmem_limit_bytes=VMEM_LIMIT),
    )(held, level_two)
    return (coarse.reshape(aggs, tile, 7 * w), level_two.reshape(1, tile, 7 * gw))


def per_device(*args):
    done = at_once(*args)
    return in_stages(*args) if done is None else done


def solution(mesh):
    placed = (
        P(("slab", "piece"), None, None),
        P(("slab", "piece"), None),
        P(("slab", "piece"), None),
        P(("slab", "piece"), None, None),
        P(("slab", "piece"), None, None),
        P(("slab", "piece")),
        P(("slab", "piece"), None, None),
        P(("slab", "piece")),
    )
    return jax.shard_map(
        per_device,
        mesh=mesh,
        in_specs=placed,
        out_specs=(P(("slab", "piece"), None, None), P(("slab", "piece"), None, None)),
        check_vma=False,
    )
```

```python
import functools

import jax
import jax.numpy as jnp
import numpy as np
from jax import lax
from jax.experimental import pallas as pl
from jax.experimental.pallas import tpu as pltpu
from jax.sharding import PartitionSpec as P

DAMPING = 2.0 / 3.0
LANES = 128
MESH = pl.DeviceIdType.MESH
VMEM_LIMIT = 60 * 1024 * 1024
FUSED_LIMIT = 52 * 1024 * 1024
F32 = jnp.float32
BF16 = jnp.bfloat16


def mm(a, b):
    return jnp.dot(a, b, preferred_element_type=F32)


def gather_kernel(n, far, a_ref, d_ref, t_ref, q_ref, i_ref, ag, dg, tg, ig, send_sem, recv_sem):
    s, p = lax.axis_index("slab"), lax.axis_index("piece")
    barrier = pltpu.get_barrier_semaphore()

    @pl.when(s > 0)
    def _():
        pl.semaphore_signal(barrier, inc=1, device_id=(s - 1, p), device_id_type=MESH)

    @pl.when(s < n - 1)
    def _():
        pl.semaphore_signal(barrier, inc=1, device_id=(s + 1, p), device_id_type=MESH)

    half = d_ref.shape[0] // 2
    ag[s] = a_ref[...]
    dg[s] = jnp.concatenate([d_ref[0:half, :], d_ref[half : 2 * half, :]], axis=1)
    tg[s] = jnp.concatenate([t_ref[...], q_ref[...]], axis=1)
    ig[s] = i_ref[...]

    peers = jnp.where(s > 0, 1, 0) + jnp.where(s < n - 1, 1, 0)
    pl.semaphore_wait(barrier, peers)

    arrays = (ig, tg, dg, ag)
    reach = (far, far, 2, 2)

    def copy(way, step, which, slab):
        there = s + 1 if way == 0 else s - 1
        return pltpu.make_async_remote_copy(
            src_ref=arrays[which].at[slab],
            dst_ref=arrays[which].at[slab],
            send_sem=send_sem.at[way, step, which],
            recv_sem=recv_sem.at[way, step, which],
            device_id=(there, p),
            device_id_type=MESH,
        )

    def sends(way, step):
        if way == 0:
            return (s - step >= 0) & (s + 1 < n), s - step
        return (s + step < n) & (s >= 1), s + step

    def gets(way, step):
        if way == 0:
            return s - 1 - step >= 0, s - 1 - step
        return s + 1 + step < n, s + 1 + step

    steps = min(far, n - 1)
    for step in range(steps + 1):
        for which in range(4):
            for way in range(2):
                if 0 < step <= min(reach[which], steps):
                    ok, slab = gets(way, step - 1)

                    @pl.when(ok)
                    def _(way=way, which=which, slab=slab):
                        copy(way, step - 1, which, slab).wait_recv()

                if step < min(reach[which], steps):
                    ok, slab = sends(way, step)

                    @pl.when(ok)
                    def _(way=way, which=which, slab=slab):
                        copy(way, step, which, slab).start()

    for step in range(steps):
        for which in range(4):
            for way in range(2):
                if step < reach[which]:
                    ok, slab = sends(way, step)

                    @pl.when(ok)
                    def _(way=way, which=which, slab=slab):
                        copy(way, step, which, slab).wait_send()


def level_kernel(
    n, blocks, slots, aggs, groups, tile, s_ref, i_ref, ag, dg, tg,
    out, cb, t2s, t2t, ad, sd, pro, ts, acc, bd, wm,
):
    s = s_ref[0]
    rows, w, gw = blocks * tile, aggs * tile, groups * tile
    pair = 2 * tile
    lane = lax.broadcasted_iota(jnp.int32, (tile, pair), 1) // tile

    for v in range(n):
        near = jnp.abs(v - s) <= 3
        for b in range(blocks):
            x = tg[v, b * tile : (b + 1) * tile, :].astype(F32)
            turned = pltpu.roll(x, tile, 1)
            one = jnp.where(lane == 0, x, turned)
            two = jnp.where(lane == 0, turned, x)
            g1 = jnp.where(near, i_ref[v, 2, b], -1)
            g2 = jnp.where(near, i_ref[v, 3, b], -1)
            for q in range(w // pair):
                ts[v, b * tile : (b + 1) * tile, q * pair : (q + 1) * pair] = jnp.where(
                    lane + 2 * q == g1, one, 0.0
                ).astype(BF16)
            for q in range(gw // pair):
                t2s[v, b * tile : (b + 1) * tile, q * pair : (q + 1) * pair] = jnp.where(
                    lane + 2 * q == g2, two, 0.0
                ).astype(BF16)

    t2t[...] = t2s[s].astype(F32).T.astype(BF16)
    bd[...] = jnp.zeros_like(bd)

    for e in range(-2, 3):
        u = s + e

        @pl.when((u >= 0) & (u < n))
        def _(e=e, u=u):
            def row(i, carry):
                acc[...] = jnp.zeros_like(acc)
                base = pl.multiple_of(i * tile, tile)
                for k2 in range(slots // 2):
                    x = ag[u, pl.ds(base, tile), k2 * pair : (k2 + 1) * pair].astype(F32)
                    turned = pltpu.roll(x, tile, 1)
                    for odd in range(2):
                        k = 2 * k2 + odd
                        c = i_ref[u, 0, i * slots + k]
                        m = i_ref[u, 1, i * slots + k]
                        side = lax.rem(c, 2)
                        y = jnp.where(side == odd, x, turned)
                        keep = jnp.where(m != 0, side, -1)
                        at = pl.multiple_of((c // 2) * pair, pair)
                        acc[:, pl.ds(at, pair)] += jnp.where(lane == keep, y, 0.0)
                ad[e + 2, pl.ds(base, tile), :] = acc[...].astype(BF16)
                return carry

            lax.fori_loop(0, blocks, row, 0)
            half = blocks // 2
            for h in range(2):
                for b in range(half):
                    x = dg[u, b * tile : (b + 1) * tile, :].astype(F32)
                    if b % 2 != h:
                        x = pltpu.roll(x, tile, 1)
                    bd[b * tile : (b + 1) * tile, (b // 2) * pair : (b // 2 + 1) * pair] = (
                        jnp.where(lane == b % 2, x, 0.0).astype(BF16)
                    )
                lo = h * half * tile
                hi = lo + half * tile
                sd[lo:hi, :] = (DAMPING * mm(bd[...], ad[e + 2, lo:hi, :])).astype(BF16)
            for j in range(3):
                v = u + j - 1
                inside = (v >= 0) & (v < n)

                @pl.when(inside)
                def _(j=j, v=v):
                    value = -mm(sd[:, j * rows : (j + 1) * rows], ts[v])
                    if j == 1:
                        value = value + ts[v].astype(F32)
                    pro[e + 2, :, j * w : (j + 1) * w] = value.astype(BF16)

                @pl.when(jnp.logical_not(inside))
                def _(j=j):
                    pro[e + 2, :, j * w : (j + 1) * w] = jnp.zeros((rows, w), BF16)

        @pl.when((u < 0) | (u >= n))
        def _(e=e):
            pro[e + 2] = jnp.zeros((rows, 3 * w), BF16)
            if abs(e) < 2:
                ad[e + 2] = jnp.zeros((rows, 3 * rows), BF16)

    turned = [pro[dj + 2, :, (1 - dj) * w : (2 - dj) * w].astype(F32).T.astype(BF16) for dj in (-1, 0, 1)]
    for e in range(-2, 3):
        total = None
        for dj in (-1, 0, 1):
            j = e - dj + 1
            if 0 <= j < 3:
                term = mm(turned[dj + 1], ad[dj + 2, :, j * rows : (j + 1) * rows])
                total = term if total is None else total + term
        wm[e + 2] = total.astype(BF16)

    short = n < 7
    for f in range(-3, 4):
        t = s + f
        inside = (t >= 0) & (t < n)

        @pl.when(inside)
        def _(f=f, t=t):
            total = None
            for e in range(max(-2, f - 1), min(2, f + 1) + 1):
                j = f - e + 1
                term = mm(wm[e + 2], pro[e + 2, :, j * w : (j + 1) * w])
                total = term if total is None else total + term
            out[:, (f + 3) * w : (f + 4) * w] = total
            cb[t if short else f + 3] = total.astype(BF16)

        @pl.when(jnp.logical_not(inside))
        def _(f=f):
            out[:, (f + 3) * w : (f + 4) * w] = jnp.zeros((w, w), F32)
            if not short:
                cb[f + 3] = jnp.zeros((w, w), BF16)


def scatter_kernel(
    n, parts, groups, tile, cb, t2s, t2t, out, term, mine, rx1, tx2, rx2,
    send1, recv1, send2, recv2,
):
    s, p = lax.axis_index("slab"), lax.axis_index("piece")
    chips = groups // 2
    odd = lax.rem(p, 2)
    chip = p // 2
    sibling = p + 1 - 2 * odd
    gw = groups * tile
    mates = [2 * lax.rem(chip + o, chips) + odd for o in range(1, chips)]

    barrier = pltpu.get_barrier_semaphore()
    for mate in [sibling] + mates:
        pl.semaphore_signal(barrier, inc=1, device_id=(s, mate), device_id_type=MESH)
    if n < 7:
        out[...] = jnp.zeros_like(out)
    pl.semaphore_wait(barrier, chips)

    def pair_copy(m):
        return pltpu.make_async_remote_copy(
            src_ref=term.at[m, 1 - odd],
            dst_ref=rx1.at[m],
            send_sem=send1.at[m],
            recv_sem=recv1.at[m],
            device_id=(s, sibling),
            device_id_type=MESH,
        )

    def chip_copy(m, o):
        return pltpu.make_async_remote_copy(
            src_ref=tx2.at[m, o - 1],
            dst_ref=rx2.at[m, o - 1],
            send_sem=send2.at[m, o - 1],
            recv_sem=recv2.at[m, o - 1],
            device_id=(s, mates[o - 1]),
            device_id_type=MESH,
        )

    def pair_sum(m):
        pair_copy(m).wait_recv()
        for o in range(1, chips):
            h = lax.rem(chip + o, chips)
            tx2[m, o - 1] = (term[m, odd, h].astype(F32) + rx1[m, h].astype(F32)).astype(BF16)
            chip_copy(m, o).start()
        mine[m] = term[m, odd, chip].astype(F32) + rx1[m, chip].astype(F32)

    for m in range(parts):
        v = m if n < 7 else jnp.clip(s + m - 3, 0, n - 1)
        left = mm(t2t[...], cb[m]).astype(BF16)
        both = mm(left, t2s[v]).astype(BF16)
        for g in range(groups):
            term[m, g % 2, g // 2] = both[g * tile : (g + 1) * tile, :]
        pair_copy(m).start()
        if m > 0:
            pair_sum(m - 1)
    pair_sum(parts - 1)
    for m in range(parts):
        total = mine[m]
        for o in range(1, chips):
            chip_copy(m, o).wait_recv()
            total = total + rx2[m, o - 1].astype(F32)
        place = (m + 3 - s) * gw if n < 7 else m * gw
        out[:, pl.ds(pl.multiple_of(place, LANES), gw)] = total
    for m in range(parts):
        pair_copy(m).wait_send()
        for o in range(1, chips):
            chip_copy(m, o).wait_send()


def in_stages(
    fine_tiles, fine_cols, bond_mask, diag_inv, tentative, aggregate, tentative_two, aggregate_two
):
    blocks, tile = diag_inv.shape[0], diag_inv.shape[1]
    slots = fine_cols.shape[1]
    aggs = tentative_two.shape[0]
    n, groups = lax.axis_size("slab"), lax.axis_size("piece")
    rows, w, gw = blocks * tile, aggs * tile, groups * tile
    parts = min(7, n)
    vmem = pl.BlockSpec(memory_space=pltpu.VMEM)
    smem = pl.BlockSpec(memory_space=pltpu.SMEM)
    shape = jax.ShapeDtypeStruct

    width = -(-blocks * slots // LANES) * LANES

    def line(x):
        x = x.reshape(1, -1)
        return jnp.pad(x, ((0, 0), (0, width - x.shape[1])))

    ints = jnp.concatenate([line(fine_cols), line(bond_mask), line(aggregate), line(aggregate_two)], 0)
    ints = jnp.pad(ints, ((0, 4), (0, 0)))

    far = min(3, n - 1)
    ag, dg, tg, ig = pl.pallas_call(
        functools.partial(gather_kernel, n, far),
        out_shape=(
            shape((n, rows, slots * tile), BF16),
            shape((n, rows // 2, 2 * tile), BF16),
            shape((n, rows, 2 * tile), BF16),
            shape((n, 8, width), jnp.int32),
        ),
        in_specs=[vmem] * 5,
        out_specs=(vmem,) * 4,
        scratch_shapes=[
            pltpu.SemaphoreType.DMA((2, far, 4)),
            pltpu.SemaphoreType.DMA((2, far, 4)),
        ],
        compiler_params=pltpu.CompilerParams(
            collective_id=0, has_side_effects=True, vmem_limit_bytes=VMEM_LIMIT
        ),
    )(
        fine_tiles.reshape(rows, slots * tile),
        diag_inv.reshape(rows, tile),
        tentative.reshape(rows, tile),
        tentative_two.reshape(w, tile),
        ints,
    )

    slab = lax.axis_index("slab").astype(jnp.int32).reshape(1)
    coarse, cb, t2s, t2t = pl.pallas_call(
        functools.partial(level_kernel, n, blocks, slots, aggs, groups, tile),
        out_shape=(
            shape((w, 7 * w), F32),
            shape((parts, w, w), BF16),
            shape((n, w, gw), BF16),
            shape((gw, w), BF16),
        ),
        in_specs=[smem, smem, vmem, vmem, vmem],
        out_specs=(vmem,) * 4,
        scratch_shapes=[
            pltpu.VMEM((5, rows, 3 * rows), BF16),
            pltpu.VMEM((rows, 3 * rows), BF16),
            pltpu.VMEM((5, rows, 3 * w), BF16),
            pltpu.VMEM((n, rows, w), BF16),
            pltpu.VMEM((tile, 3 * rows), F32),
            pltpu.VMEM((rows // 2, rows // 2), BF16),
            pltpu.VMEM((5, w, rows), BF16),
        ],
        compiler_params=pltpu.CompilerParams(vmem_limit_bytes=VMEM_LIMIT),
    )(slab, ig, ag, dg, tg)

    chips = groups // 2
    level_two = pl.pallas_call(
        functools.partial(scatter_kernel, n, parts, groups, tile),
        out_shape=shape((tile, 7 * gw), F32),
        in_specs=[vmem] * 3,
        out_specs=vmem,
        scratch_shapes=[
            pltpu.VMEM((parts, 2, chips, tile, gw), BF16),
            pltpu.VMEM((parts, tile, gw), F32),
            pltpu.VMEM((parts, chips, tile, gw), BF16),
            pltpu.VMEM((parts, chips - 1, tile, gw), BF16),
            pltpu.VMEM((parts, chips - 1, tile, gw), BF16),
            pltpu.SemaphoreType.DMA((parts,)),
            pltpu.SemaphoreType.DMA((parts,)),
            pltpu.SemaphoreType.DMA((parts, chips - 1)),
            pltpu.SemaphoreType.DMA((parts, chips - 1)),
        ],
        compiler_params=pltpu.CompilerParams(
            collective_id=1, has_side_effects=True, vmem_limit_bytes=VMEM_LIMIT
        ),
    )(cb, t2s, t2t)

    return (coarse.reshape(aggs, tile, 7 * w), level_two.reshape(1, tile, 7 * gw))


def whole_kernel(
    n, blocks, slots, aggs, groups, tile,
    a_ref, d_ref, t_ref, q_ref, cols_ref, mask_ref, one_ref, two_ref, out, two,
    ag, dg, tg, cg, ad, sd, pro, ts, t2s, t2t, hot, bd, wm, cf, term, mine, rx1, tx2, rx2,
    send_sem, recv_sem, out_sem, send1, recv1, send2, recv2,
):
    s, p = lax.axis_index("slab"), lax.axis_index("piece")
    far = min(3, n - 1)
    rows, w, gw = blocks * tile, aggs * tile, groups * tile
    pair, half = 2 * tile, blocks // 2
    chips = groups // 2
    odd, chip = lax.rem(p, 2), p // 2
    sibling = p + 1 - 2 * odd
    mates = [2 * lax.rem(chip + o, chips) + odd for o in range(1, chips)]
    barrier = pltpu.get_barrier_semaphore()

    @pl.when(s > 0)
    def _():
        pl.semaphore_signal(barrier, inc=1, device_id=(s - 1, p), device_id_type=MESH)

    @pl.when(s < n - 1)
    def _():
        pl.semaphore_signal(barrier, inc=1, device_id=(s + 1, p), device_id_type=MESH)

    for mate in [sibling] + mates:
        pl.semaphore_signal(barrier, inc=1, device_id=(s, mate), device_id_type=MESH)

    line = lax.broadcasted_iota(jnp.int32, cg.shape[1:], 0)
    spot = lax.broadcasted_iota(jnp.int32, cg.shape[1:], 1)
    packed = jnp.zeros(cg.shape[1:], jnp.int32)
    for i in range(blocks):
        column = jnp.zeros(cg.shape[1:], jnp.int32)
        for k in range(slots):
            code = jnp.where(mask_ref[i, k] != 0, cols_ref[i, k], -1)
            column = jnp.where(line == k, code, column)
        column = jnp.where(line == slots, one_ref[i], column)
        column = jnp.where(line == slots + 1, two_ref[i], column)
        packed = jnp.where(spot == i, column, packed)
    cg[s] = packed.astype(F32).astype(BF16)
    tg[s] = jnp.concatenate([t_ref[...], q_ref[...]], axis=1)
    dg[s] = jnp.concatenate([d_ref[0 : rows // 2, :], d_ref[rows // 2 : rows, :]], axis=1)
    ag[s] = a_ref[...]
    peers = chips + jnp.where(s > 0, 1, 0) + jnp.where(s < n - 1, 1, 0)
    pl.semaphore_wait(barrier, peers)

    kinds = 5
    reach = (far, far) + (min(2, far),) * 3

    def part_of(which, slab):
        if which < 3:
            return (cg, tg, dg)[which].at[slab]
        return ag.at[slab, pl.ds((which - 3) * (rows // 2), rows // 2)]

    def valid(e):
        return (s + e >= 0) & (s + e < n)

    def copy(way, step, which, slab):
        return pltpu.make_async_remote_copy(
            src_ref=part_of(which, slab),
            dst_ref=part_of(which, slab),
            send_sem=send_sem.at[way, step, which],
            recv_sem=recv_sem.at[way, step, which],
            device_id=(s + 1 if way == 0 else s - 1, p),
            device_id_type=MESH,
        )

    def send(way, step, which, act):
        if step >= reach[which]:
            return
        slab = s - step if way == 0 else s + step
        ok = valid(-step) & valid(1) if way == 0 else valid(step) & valid(-1)

        @pl.when(ok)
        def _():
            act(copy(way, step, which, slab))

    def start(c):
        c.start()

    def take(e, which):
        if abs(e) > reach[which]:
            return
        way, step = (0 if e < 0 else 1), abs(e) - 1

        @pl.when(valid(e))
        def _():
            copy(way, step, which, s + e).wait_recv()

        send(way, step + 1, which, start)

    for which in range(kinds):
        for way in range(2):
            send(way, 0, which, start)

    lane = lax.broadcasted_iota(jnp.int32, (tile, pair), 1) // tile
    lane_f = lane.astype(F32)

    def basis(e):
        @pl.when(valid(e))
        def _():
            u = s + e
            names = cg[u].astype(F32)
            for b in range(blocks):
                x = tg[u, b * tile : (b + 1) * tile, :].astype(F32)
                turned = pltpu.roll(x, tile, 1)
                two_t = jnp.where(lane == 0, turned, x)
                one_t = jnp.where(lane == 0, x, turned)
                g1 = jnp.broadcast_to(names[slots : slots + 1, b : b + 1], (1, pair))
                for q in range(w // pair):
                    ts[u, b * tile : (b + 1) * tile, q * pair : (q + 1) * pair] = jnp.where(
                        lane_f + 2.0 * q == g1, one_t, 0.0
                    ).astype(BF16)
                g2 = jnp.broadcast_to(names[slots + 1 : slots + 2, b : b + 1], (1, pair))
                for q in range(gw // pair):
                    t2s[u, b * tile : (b + 1) * tile, q * pair : (q + 1) * pair] = jnp.where(
                        lane_f + 2.0 * q == g2, two_t, 0.0
                    ).astype(BF16)

    def build(e, h):
        lo, hi = h * half * tile, (h + 1) * half * tile

        @pl.when(valid(e))
        def _():
            u = s + e
            if h == 0:
                codes = cg[u].astype(F32)
                at = lax.broadcasted_iota(jnp.int32, (slots, pair), 1) // tile
                at = at.astype(F32)
                for i in range(blocks):
                    code = jnp.broadcast_to(codes[0:slots, i : i + 1], (slots, pair))
                    for cp in range(3 * rows // pair):
                        hot[i, :, cp * pair : (cp + 1) * pair] = jnp.where(
                            code == at + 2.0 * cp, 1.0, 0.0
                        )

            def row(i, carry):
                base = pl.multiple_of(i * tile, tile)
                tiles = []
                for k2 in range(slots // 2):
                    x = ag[u, pl.ds(base, tile), k2 * pair : (k2 + 1) * pair].astype(F32)
                    turned = pltpu.roll(x, tile, 1)
                    for y in (jnp.where(lane == 0, x, turned), jnp.where(lane == 0, turned, x)):
                        tiles.append(y.astype(BF16).reshape(tile // 16, 16, pair))
                for cp in range(3 * rows // pair):
                    total = None
                    for k in range(slots):
                        m = hot[i, k : k + 1, cp * pair : (cp + 1) * pair]
                        m = jnp.broadcast_to(m, (16, pair)).astype(BF16)
                        y = tiles[k] * m[None]
                        total = y if total is None else total + y
                    ad[e + 2, pl.ds(base, tile), cp * pair : (cp + 1) * pair] = total.reshape(tile, pair)
                return carry

            lax.fori_loop(h * half, (h + 1) * half, row, 0)
            for b in range(half):
                x = dg[u, b * tile : (b + 1) * tile, :].astype(F32)
                if b % 2 != h:
                    x = pltpu.roll(x, tile, 1)
                bd[b * tile : (b + 1) * tile, (b // 2) * pair : (b // 2 + 1) * pair] = (
                    jnp.where(lane == b % 2, x, 0.0).astype(BF16)
                )
            sd[lo:hi, :] = (DAMPING * mm(bd[...], ad[e + 2, lo:hi, :])).astype(BF16)

        if abs(e) < 2:

            @pl.when(jnp.logical_not(valid(e)))
            def _():
                ad[e + 2, lo:hi, :] = jnp.zeros((hi - lo, 3 * rows), BF16)

    def prolong(e, j, lo, hi):
        ok = valid(e) & valid(e + j - 1)

        @pl.when(ok)
        def _():
            v = s + e + j - 1
            value = -mm(sd[lo:hi, j * rows : (j + 1) * rows], ts[v])
            if j == 1:
                value = value + ts[v, lo:hi, :].astype(F32)
            pro[e + 2, lo:hi, j * w : (j + 1) * w] = value.astype(BF16)

        @pl.when(jnp.logical_not(ok))
        def _():
            pro[e + 2, lo:hi, j * w : (j + 1) * w] = jnp.zeros((hi - lo, w), BF16)

    def pair_copy(m):
        return pltpu.make_async_remote_copy(
            src_ref=term.at[m, 1 - odd],
            dst_ref=rx1.at[m],
            send_sem=send1.at[m],
            recv_sem=recv1.at[m],
            device_id=(s, sibling),
            device_id_type=MESH,
        )

    def chip_copy(m, o):
        return pltpu.make_async_remote_copy(
            src_ref=tx2.at[m, o - 1],
            dst_ref=rx2.at[m, o - 1],
            send_sem=send2.at[m, o - 1],
            recv_sem=recv2.at[m, o - 1],
            device_id=(s, mates[o - 1]),
            device_id_type=MESH,
        )

    def leave(f):
        return pltpu.make_async_copy(
            cf.at[f + 3], out.at[s + f if n < 7 else f + 3], out_sem.at[f + 3]
        )

    def sum_over(f, sides):
        total = None
        for e in sides:
            j = f - e + 1
            part = mm(wm[e + 2], pro[e + 2, :, j * w : (j + 1) * w])
            total = part if total is None else total + part
        return total

    def early(f):
        sides = [e for e in (-1, 0, 1) if abs(f - e) < 2]

        @pl.when(valid(f))
        def _():
            cf[f + 3] = sum_over(f, sides)

    def coarse(f):
        m = f + 3

        @pl.when(valid(f))
        def _():
            if abs(f) == 3:
                cf[m] = sum_over(f, [2 if f > 0 else -2])
            elif f != 0:
                cf[m] += sum_over(f, [2 if f > 0 else -2])
            leave(f).start()
            left = mm(t2t[...], cf[m].astype(BF16)).astype(BF16)
            both = mm(left, t2s[s + f]).astype(BF16)
            for g in range(groups):
                term[m, g % 2, g // 2] = both[g * tile : (g + 1) * tile, :]
            pair_copy(m).start()

    def pair_sum(f):
        m = f + 3

        @pl.when(valid(f))
        def _():
            pair_copy(m).wait_recv()
            for o in range(1, chips):
                h = lax.rem(chip + o, chips)
                tx2[m, o - 1] = (term[m, odd, h].astype(F32) + rx1[m, h].astype(F32)).astype(BF16)
                chip_copy(m, o).start()
            mine[m] = term[m, odd, chip].astype(F32) + rx1[m, chip].astype(F32)

    bd[...] = jnp.zeros_like(bd)
    for f in range(-3, 4):

        @pl.when(jnp.logical_not(valid(f)))
        def _(f=f):
            two[:, (f + 3) * gw : (f + 4) * gw] = jnp.zeros((tile, gw), F32)

    basis(0)
    t2t[...] = t2s[s].astype(F32).T.astype(BF16)
    build(0, 0)
    build(0, 1)
    for e in (-1, 1):
        take(e, 0)
        take(e, 1)
        basis(e)
    for j in range(3):
        prolong(0, j, 0, rows)
    for h in range(2):
        for e in (-1, 1):
            if h == 0:
                take(e, 2)
            take(e, 3 + h)
    for e in (-2, 2):
        take(e, 0)
        take(e, 1)
        basis(e)
    for e in (-1, 1):
        build(e, 0)
        build(e, 1)
        for j in range(3):
            prolong(e, j, 0, rows)
    turned = [
        pro[dj + 2, :, (1 - dj) * w : (2 - dj) * w].astype(F32).T.astype(BF16) for dj in (-1, 0, 1)
    ]
    for e in range(-2, 3):
        total = None
        for dj in (-1, 0, 1):
            j = e - dj + 1
            if 0 <= j < 3:
                part = mm(turned[dj + 1], ad[dj + 2, :, j * rows : (j + 1) * rows])
                total = part if total is None else total + part
        wm[e + 2] = total.astype(BF16)
    early(0)
    coarse(0)
    for f in (-2, -1, 1, 2):
        early(f)
    pair_sum(0)
    for e in (-3, 3):
        take(e, 0)
        take(e, 1)
        basis(e)
    order = [0]
    for way in (-1, 1):
        e = 2 * way
        take(e, 2)
        take(e, 3)
        build(e, 0)
        for j in range(3):
            prolong(e, j, 0, rows // 2)
        take(e, 4)
        build(e, 1)
        for f in (way, 2 * way, 3 * way):
            prolong(e, f - e + 1, rows // 2, rows)
            coarse(f)
            if order[-1] != 0:
                pair_sum(order[-1])
            order.append(f)
    pair_sum(order[-1])
    for f in order:
        m = f + 3

        @pl.when(valid(f))
        def _(m=m):
            total = mine[m]
            for o in range(1, chips):
                chip_copy(m, o).wait_recv()
                total = total + rx2[m, o - 1].astype(F32)
            two[:, m * gw : (m + 1) * gw] = total

    for f in range(-3, 4):
        m = f + 3

        @pl.when(valid(f))
        def _(f=f, m=m):
            leave(f).wait()
            pair_copy(m).wait_send()
            for o in range(1, chips):
                chip_copy(m, o).wait_send()

    for step in range(far):
        for which in range(kinds):
            for way in range(2):
                send(way, step, which, lambda c: c.wait_send())


def place_kernel(n, blocks, level, out, two, zero, sem, last):
    s = lax.axis_index("slab")
    cut, w = zero.shape
    parts = w // cut
    other = pltpu.make_async_copy(level, two, last)
    other.start()
    zero[...] = jnp.zeros_like(zero)

    def each(act):
        for f in range(-3, 4):
            ok = (s + f >= 0) & (s + f < n)
            for q in range(parts):
                to = out.at[pl.ds(q * cut, cut), pl.ds((f + 3) * w, w)]

                @pl.when(ok)
                def _(f=f, q=q, to=to):
                    slab = s + f if n < 7 else f + 3
                    have = blocks.at[slab, pl.ds(q * cut, cut)]
                    act(pltpu.make_async_copy(have, to, sem.at[f + 3, q]))

                @pl.when(jnp.logical_not(ok))
                def _(f=f, q=q, to=to):
                    act(pltpu.make_async_copy(zero, to, sem.at[f + 3, q]))

    each(lambda c: c.start())
    each(lambda c: c.wait())
    other.wait()


def at_once(
    fine_tiles, fine_cols, bond_mask, diag_inv, tentative, aggregate, tentative_two, aggregate_two
):
    blocks, tile = diag_inv.shape[0], diag_inv.shape[1]
    slots = fine_cols.shape[1]
    aggs = tentative_two.shape[0]
    n, groups = lax.axis_size("slab"), lax.axis_size("piece")
    rows, w, gw = blocks * tile, aggs * tile, groups * tile
    pair, chips, far = 2 * tile, groups // 2, min(3, n - 1)
    names = -(-(slots + 2) // 16) * 16
    kept = min(n, 7)
    vmem = pl.BlockSpec(memory_space=pltpu.VMEM)
    smem = pl.BlockSpec(memory_space=pltpu.SMEM)
    dma = pltpu.SemaphoreType.DMA
    scratch = [
        pltpu.VMEM((n, rows, slots * tile), BF16),
        pltpu.VMEM((n, rows // 2, pair), BF16),
        pltpu.VMEM((n, rows, pair), BF16),
        pltpu.VMEM((n, names, LANES), BF16),
        pltpu.VMEM((5, rows, 3 * rows), BF16),
        pltpu.VMEM((rows, 3 * rows), BF16),
        pltpu.VMEM((5, rows, 3 * w), BF16),
        pltpu.VMEM((n, rows, w), BF16),
        pltpu.VMEM((n, w, gw), BF16),
        pltpu.VMEM((gw, w), BF16),
        pltpu.VMEM((blocks, slots, 3 * rows), F32),
        pltpu.VMEM((rows // 2, rows // 2), BF16),
        pltpu.VMEM((5, w, rows), BF16),
        pltpu.VMEM((7, w, w), F32),
        pltpu.VMEM((7, 2, chips, tile, gw), BF16),
        pltpu.VMEM((7, tile, gw), F32),
        pltpu.VMEM((7, chips, tile, gw), BF16),
        pltpu.VMEM((7, chips - 1, tile, gw), BF16),
        pltpu.VMEM((7, chips - 1, tile, gw), BF16),
    ]
    size = sum(x.dtype.itemsize * np.prod(x.shape) for x in scratch)
    if size > 0.92 * FUSED_LIMIT:
        return None
    held, level_two = pl.pallas_call(
        functools.partial(whole_kernel, n, blocks, slots, aggs, groups, tile),
        out_shape=(
            jax.ShapeDtypeStruct((kept, w, w), F32),
            jax.ShapeDtypeStruct((tile, 7 * gw), F32),
        ),
        in_specs=[vmem] * 4 + [smem] * 4,
        out_specs=(pl.BlockSpec(memory_space=pl.ANY), vmem),
        scratch_shapes=scratch
        + [
            dma((2, far, 5)),
            dma((2, far, 5)),
            dma((7,)),
            dma((7,)),
            dma((7,)),
            dma((7, chips - 1)),
            dma((7, chips - 1)),
        ],
        compiler_params=pltpu.CompilerParams(
            collective_id=2, has_side_effects=True, vmem_limit_bytes=FUSED_LIMIT
        ),
    )(
        fine_tiles.reshape(rows, slots * tile),
        diag_inv.reshape(rows, tile),
        tentative.reshape(rows, tile),
        tentative_two.reshape(w, tile),
        fine_cols,
        bond_mask,
        aggregate,
        aggregate_two,
    )
    coarse, level_two = pl.pallas_call(
        functools.partial(place_kernel, n),
        out_shape=(
            jax.ShapeDtypeStruct((w, 7 * w), F32),
            jax.ShapeDtypeStruct((tile, 7 * gw), F32),
        ),
        in_specs=[pl.BlockSpec(memory_space=pl.ANY)] * 2,
        out_specs=(pl.BlockSpec(memory_space=pl.ANY),) * 2,
        scratch_shapes=[
            pltpu.VMEM((w // 4, w), F32),
            dma((7, 4)),
            dma(()),
        ],
        compiler_params=pltpu.CompilerParams(vmem_limit_bytes=4 * 1024 * 1024),
    )(held, level_two)
    return (coarse.reshape(aggs, tile, 7 * w), level_two.reshape(1, tile, 7 * gw))


def per_device(*args):
    done = at_once(*args)
    return in_stages(*args) if done is None else done


def solution(mesh):
    placed = (
        P(("slab", "piece"), None, None),
        P(("slab", "piece"), None),
        P(("slab", "piece"), None),
        P(("slab", "piece"), None, None),
        P(("slab", "piece"), None, None),
        P(("slab", "piece")),
        P(("slab", "piece"), None, None),
        P(("slab", "piece")),
    )
    return jax.shard_map(
        per_device,
        mesh=mesh,
        in_specs=placed,
        out_specs=(P(("slab", "piece"), None, None), P(("slab", "piece"), None, None)),
        check_vma=False,
    )
```

```python
import functools

import jax
import jax.numpy as jnp
import numpy as np
from jax import lax
from jax.experimental import pallas as pl
from jax.experimental.pallas import tpu as pltpu
from jax.sharding import PartitionSpec as P

DAMPING = 2.0 / 3.0
LANES = 128
MESH = pl.DeviceIdType.MESH
VMEM_LIMIT = 60 * 1024 * 1024
FUSED_LIMIT = 52 * 1024 * 1024
F32 = jnp.float32
BF16 = jnp.bfloat16


def mm(a, b):
    return jnp.dot(a, b, preferred_element_type=F32)


def gather_kernel(n, far, a_ref, d_ref, t_ref, q_ref, i_ref, ag, dg, tg, ig, send_sem, recv_sem):
    s, p = lax.axis_index("slab"), lax.axis_index("piece")
    barrier = pltpu.get_barrier_semaphore()

    @pl.when(s > 0)
    def _():
        pl.semaphore_signal(barrier, inc=1, device_id=(s - 1, p), device_id_type=MESH)

    @pl.when(s < n - 1)
    def _():
        pl.semaphore_signal(barrier, inc=1, device_id=(s + 1, p), device_id_type=MESH)

    half = d_ref.shape[0] // 2
    ag[s] = a_ref[...]
    dg[s] = jnp.concatenate([d_ref[0:half, :], d_ref[half : 2 * half, :]], axis=1)
    tg[s] = jnp.concatenate([t_ref[...], q_ref[...]], axis=1)
    ig[s] = i_ref[...]

    peers = jnp.where(s > 0, 1, 0) + jnp.where(s < n - 1, 1, 0)
    pl.semaphore_wait(barrier, peers)

    arrays = (ig, tg, dg, ag)
    reach = (far, far, 2, 2)

    def copy(way, step, which, slab):
        there = s + 1 if way == 0 else s - 1
        return pltpu.make_async_remote_copy(
            src_ref=arrays[which].at[slab],
            dst_ref=arrays[which].at[slab],
            send_sem=send_sem.at[way, step, which],
            recv_sem=recv_sem.at[way, step, which],
            device_id=(there, p),
            device_id_type=MESH,
        )

    def sends(way, step):
        if way == 0:
            return (s - step >= 0) & (s + 1 < n), s - step
        return (s + step < n) & (s >= 1), s + step

    def gets(way, step):
        if way == 0:
            return s - 1 - step >= 0, s - 1 - step
        return s + 1 + step < n, s + 1 + step

    steps = min(far, n - 1)
    for step in range(steps + 1):
        for which in range(4):
            for way in range(2):
                if 0 < step <= min(reach[which], steps):
                    ok, slab = gets(way, step - 1)

                    @pl.when(ok)
                    def _(way=way, which=which, slab=slab):
                        copy(way, step - 1, which, slab).wait_recv()

                if step < min(reach[which], steps):
                    ok, slab = sends(way, step)

                    @pl.when(ok)
                    def _(way=way, which=which, slab=slab):
                        copy(way, step, which, slab).start()

    for step in range(steps):
        for which in range(4):
            for way in range(2):
                if step < reach[which]:
                    ok, slab = sends(way, step)

                    @pl.when(ok)
                    def _(way=way, which=which, slab=slab):
                        copy(way, step, which, slab).wait_send()


def level_kernel(
    n, blocks, slots, aggs, groups, tile, s_ref, i_ref, ag, dg, tg,
    out, cb, t2s, t2t, ad, sd, pro, ts, acc, bd, wm,
):
    s = s_ref[0]
    rows, w, gw = blocks * tile, aggs * tile, groups * tile
    pair = 2 * tile
    lane = lax.broadcasted_iota(jnp.int32, (tile, pair), 1) // tile

    for v in range(n):
        near = jnp.abs(v - s) <= 3
        for b in range(blocks):
            x = tg[v, b * tile : (b + 1) * tile, :].astype(F32)
            turned = pltpu.roll(x, tile, 1)
            one = jnp.where(lane == 0, x, turned)
            two = jnp.where(lane == 0, turned, x)
            g1 = jnp.where(near, i_ref[v, 2, b], -1)
            g2 = jnp.where(near, i_ref[v, 3, b], -1)
            for q in range(w // pair):
                ts[v, b * tile : (b + 1) * tile, q * pair : (q + 1) * pair] = jnp.where(
                    lane + 2 * q == g1, one, 0.0
                ).astype(BF16)
            for q in range(gw // pair):
                t2s[v, b * tile : (b + 1) * tile, q * pair : (q + 1) * pair] = jnp.where(
                    lane + 2 * q == g2, two, 0.0
                ).astype(BF16)

    t2t[...] = t2s[s].astype(F32).T.astype(BF16)
    bd[...] = jnp.zeros_like(bd)

    for e in range(-2, 3):
        u = s + e

        @pl.when((u >= 0) & (u < n))
        def _(e=e, u=u):
            def row(i, carry):
                acc[...] = jnp.zeros_like(acc)
                base = pl.multiple_of(i * tile, tile)
                for k2 in range(slots // 2):
                    x = ag[u, pl.ds(base, tile), k2 * pair : (k2 + 1) * pair].astype(F32)
                    turned = pltpu.roll(x, tile, 1)
                    for odd in range(2):
                        k = 2 * k2 + odd
                        c = i_ref[u, 0, i * slots + k]
                        m = i_ref[u, 1, i * slots + k]
                        side = lax.rem(c, 2)
                        y = jnp.where(side == odd, x, turned)
                        keep = jnp.where(m != 0, side, -1)
                        at = pl.multiple_of((c // 2) * pair, pair)
                        acc[:, pl.ds(at, pair)] += jnp.where(lane == keep, y, 0.0)
                ad[e + 2, pl.ds(base, tile), :] = acc[...].astype(BF16)
                return carry

            lax.fori_loop(0, blocks, row, 0)
            half = blocks // 2
            for h in range(2):
                for b in range(half):
                    x = dg[u, b * tile : (b + 1) * tile, :].astype(F32)
                    if b % 2 != h:
                        x = pltpu.roll(x, tile, 1)
                    bd[b * tile : (b + 1) * tile, (b // 2) * pair : (b // 2 + 1) * pair] = (
                        jnp.where(lane == b % 2, x, 0.0).astype(BF16)
                    )
                lo = h * half * tile
                hi = lo + half * tile
                sd[lo:hi, :] = (DAMPING * mm(bd[...], ad[e + 2, lo:hi, :])).astype(BF16)
            for j in range(3):
                v = u + j - 1
                inside = (v >= 0) & (v < n)

                @pl.when(inside)
                def _(j=j, v=v):
                    value = -mm(sd[:, j * rows : (j + 1) * rows], ts[v])
                    if j == 1:
                        value = value + ts[v].astype(F32)
                    pro[e + 2, :, j * w : (j + 1) * w] = value.astype(BF16)

                @pl.when(jnp.logical_not(inside))
                def _(j=j):
                    pro[e + 2, :, j * w : (j + 1) * w] = jnp.zeros((rows, w), BF16)

        @pl.when((u < 0) | (u >= n))
        def _(e=e):
            pro[e + 2] = jnp.zeros((rows, 3 * w), BF16)
            if abs(e) < 2:
                ad[e + 2] = jnp.zeros((rows, 3 * rows), BF16)

    turned = [pro[dj + 2, :, (1 - dj) * w : (2 - dj) * w].astype(F32).T.astype(BF16) for dj in (-1, 0, 1)]
    for e in range(-2, 3):
        total = None
        for dj in (-1, 0, 1):
            j = e - dj + 1
            if 0 <= j < 3:
                term = mm(turned[dj + 1], ad[dj + 2, :, j * rows : (j + 1) * rows])
                total = term if total is None else total + term
        wm[e + 2] = total.astype(BF16)

    short = n < 7
    for f in range(-3, 4):
        t = s + f
        inside = (t >= 0) & (t < n)

        @pl.when(inside)
        def _(f=f, t=t):
            total = None
            for e in range(max(-2, f - 1), min(2, f + 1) + 1):
                j = f - e + 1
                term = mm(wm[e + 2], pro[e + 2, :, j * w : (j + 1) * w])
                total = term if total is None else total + term
            out[:, (f + 3) * w : (f + 4) * w] = total
            cb[t if short else f + 3] = total.astype(BF16)

        @pl.when(jnp.logical_not(inside))
        def _(f=f):
            out[:, (f + 3) * w : (f + 4) * w] = jnp.zeros((w, w), F32)
            if not short:
                cb[f + 3] = jnp.zeros((w, w), BF16)


def scatter_kernel(
    n, parts, groups, tile, cb, t2s, t2t, out, term, mine, rx1, tx2, rx2,
    send1, recv1, send2, recv2,
):
    s, p = lax.axis_index("slab"), lax.axis_index("piece")
    chips = groups // 2
    odd = lax.rem(p, 2)
    chip = p // 2
    sibling = p + 1 - 2 * odd
    gw = groups * tile
    mates = [2 * lax.rem(chip + o, chips) + odd for o in range(1, chips)]

    barrier = pltpu.get_barrier_semaphore()
    for mate in [sibling] + mates:
        pl.semaphore_signal(barrier, inc=1, device_id=(s, mate), device_id_type=MESH)
    if n < 7:
        out[...] = jnp.zeros_like(out)
    pl.semaphore_wait(barrier, chips)

    def pair_copy(m):
        return pltpu.make_async_remote_copy(
            src_ref=term.at[m, 1 - odd],
            dst_ref=rx1.at[m],
            send_sem=send1.at[m],
            recv_sem=recv1.at[m],
            device_id=(s, sibling),
            device_id_type=MESH,
        )

    def chip_copy(m, o):
        return pltpu.make_async_remote_copy(
            src_ref=tx2.at[m, o - 1],
            dst_ref=rx2.at[m, o - 1],
            send_sem=send2.at[m, o - 1],
            recv_sem=recv2.at[m, o - 1],
            device_id=(s, mates[o - 1]),
            device_id_type=MESH,
        )

    def pair_sum(m):
        pair_copy(m).wait_recv()
        for o in range(1, chips):
            h = lax.rem(chip + o, chips)
            tx2[m, o - 1] = (term[m, odd, h].astype(F32) + rx1[m, h].astype(F32)).astype(BF16)
            chip_copy(m, o).start()
        mine[m] = term[m, odd, chip].astype(F32) + rx1[m, chip].astype(F32)

    for m in range(parts):
        v = m if n < 7 else jnp.clip(s + m - 3, 0, n - 1)
        left = mm(t2t[...], cb[m]).astype(BF16)
        both = mm(left, t2s[v]).astype(BF16)
        for g in range(groups):
            term[m, g % 2, g // 2] = both[g * tile : (g + 1) * tile, :]
        pair_copy(m).start()
        if m > 0:
            pair_sum(m - 1)
    pair_sum(parts - 1)
    for m in range(parts):
        total = mine[m]
        for o in range(1, chips):
            chip_copy(m, o).wait_recv()
            total = total + rx2[m, o - 1].astype(F32)
        place = (m + 3 - s) * gw if n < 7 else m * gw
        out[:, pl.ds(pl.multiple_of(place, LANES), gw)] = total
    for m in range(parts):
        pair_copy(m).wait_send()
        for o in range(1, chips):
            chip_copy(m, o).wait_send()


def in_stages(
    fine_tiles, fine_cols, bond_mask, diag_inv, tentative, aggregate, tentative_two, aggregate_two
):
    blocks, tile = diag_inv.shape[0], diag_inv.shape[1]
    slots = fine_cols.shape[1]
    aggs = tentative_two.shape[0]
    n, groups = lax.axis_size("slab"), lax.axis_size("piece")
    rows, w, gw = blocks * tile, aggs * tile, groups * tile
    parts = min(7, n)
    vmem = pl.BlockSpec(memory_space=pltpu.VMEM)
    smem = pl.BlockSpec(memory_space=pltpu.SMEM)
    shape = jax.ShapeDtypeStruct

    width = -(-blocks * slots // LANES) * LANES

    def line(x):
        x = x.reshape(1, -1)
        return jnp.pad(x, ((0, 0), (0, width - x.shape[1])))

    ints = jnp.concatenate([line(fine_cols), line(bond_mask), line(aggregate), line(aggregate_two)], 0)
    ints = jnp.pad(ints, ((0, 4), (0, 0)))

    far = min(3, n - 1)
    ag, dg, tg, ig = pl.pallas_call(
        functools.partial(gather_kernel, n, far),
        out_shape=(
            shape((n, rows, slots * tile), BF16),
            shape((n, rows // 2, 2 * tile), BF16),
            shape((n, rows, 2 * tile), BF16),
            shape((n, 8, width), jnp.int32),
        ),
        in_specs=[vmem] * 5,
        out_specs=(vmem,) * 4,
        scratch_shapes=[
            pltpu.SemaphoreType.DMA((2, far, 4)),
            pltpu.SemaphoreType.DMA((2, far, 4)),
        ],
        compiler_params=pltpu.CompilerParams(
            collective_id=0, has_side_effects=True, vmem_limit_bytes=VMEM_LIMIT
        ),
    )(
        fine_tiles.reshape(rows, slots * tile),
        diag_inv.reshape(rows, tile),
        tentative.reshape(rows, tile),
        tentative_two.reshape(w, tile),
        ints,
    )

    slab = lax.axis_index("slab").astype(jnp.int32).reshape(1)
    coarse, cb, t2s, t2t = pl.pallas_call(
        functools.partial(level_kernel, n, blocks, slots, aggs, groups, tile),
        out_shape=(
            shape((w, 7 * w), F32),
            shape((parts, w, w), BF16),
            shape((n, w, gw), BF16),
            shape((gw, w), BF16),
        ),
        in_specs=[smem, smem, vmem, vmem, vmem],
        out_specs=(vmem,) * 4,
        scratch_shapes=[
            pltpu.VMEM((5, rows, 3 * rows), BF16),
            pltpu.VMEM((rows, 3 * rows), BF16),
            pltpu.VMEM((5, rows, 3 * w), BF16),
            pltpu.VMEM((n, rows, w), BF16),
            pltpu.VMEM((tile, 3 * rows), F32),
            pltpu.VMEM((rows // 2, rows // 2), BF16),
            pltpu.VMEM((5, w, rows), BF16),
        ],
        compiler_params=pltpu.CompilerParams(vmem_limit_bytes=VMEM_LIMIT),
    )(slab, ig, ag, dg, tg)

    chips = groups // 2
    level_two = pl.pallas_call(
        functools.partial(scatter_kernel, n, parts, groups, tile),
        out_shape=shape((tile, 7 * gw), F32),
        in_specs=[vmem] * 3,
        out_specs=vmem,
        scratch_shapes=[
            pltpu.VMEM((parts, 2, chips, tile, gw), BF16),
            pltpu.VMEM((parts, tile, gw), F32),
            pltpu.VMEM((parts, chips, tile, gw), BF16),
            pltpu.VMEM((parts, chips - 1, tile, gw), BF16),
            pltpu.VMEM((parts, chips - 1, tile, gw), BF16),
            pltpu.SemaphoreType.DMA((parts,)),
            pltpu.SemaphoreType.DMA((parts,)),
            pltpu.SemaphoreType.DMA((parts, chips - 1)),
            pltpu.SemaphoreType.DMA((parts, chips - 1)),
        ],
        compiler_params=pltpu.CompilerParams(
            collective_id=1, has_side_effects=True, vmem_limit_bytes=VMEM_LIMIT
        ),
    )(cb, t2s, t2t)

    return (coarse.reshape(aggs, tile, 7 * w), level_two.reshape(1, tile, 7 * gw))


def whole_kernel(
    n, blocks, slots, aggs, groups, tile,
    a_ref, d_ref, t_ref, q_ref, cols_ref, mask_ref, one_ref, two_ref, out, two,
    ag, dg, tg, cg, ad, sd, pro, ts, t2s, t2t, hot, bd, wm, cf, term, mine, rx1, tx2, rx2,
    send_sem, recv_sem, out_sem, send1, recv1, send2, recv2,
):
    s, p = lax.axis_index("slab"), lax.axis_index("piece")
    far = min(3, n - 1)
    rows, w, gw = blocks * tile, aggs * tile, groups * tile
    pair, half = 2 * tile, blocks // 2
    chips = groups // 2
    odd, chip = lax.rem(p, 2), p // 2
    sibling = p + 1 - 2 * odd
    mates = [2 * lax.rem(chip + o, chips) + odd for o in range(1, chips)]
    barrier = pltpu.get_barrier_semaphore()

    @pl.when(s > 0)
    def _():
        pl.semaphore_signal(barrier, inc=1, device_id=(s - 1, p), device_id_type=MESH)

    @pl.when(s < n - 1)
    def _():
        pl.semaphore_signal(barrier, inc=1, device_id=(s + 1, p), device_id_type=MESH)

    for mate in [sibling] + mates:
        pl.semaphore_signal(barrier, inc=1, device_id=(s, mate), device_id_type=MESH)

    line = lax.broadcasted_iota(jnp.int32, cg.shape[1:], 0)
    spot = lax.broadcasted_iota(jnp.int32, cg.shape[1:], 1)
    packed = jnp.zeros(cg.shape[1:], jnp.int32)
    for i in range(blocks):
        column = jnp.zeros(cg.shape[1:], jnp.int32)
        for k in range(slots):
            code = jnp.where(mask_ref[i, k] != 0, cols_ref[i, k], -1)
            column = jnp.where(line == k, code, column)
        column = jnp.where(line == slots, one_ref[i], column)
        column = jnp.where(line == slots + 1, two_ref[i], column)
        packed = jnp.where(spot == i, column, packed)
    cg[s] = packed.astype(F32).astype(BF16)
    tg[s] = jnp.concatenate([t_ref[...], q_ref[...]], axis=1)
    dg[s] = jnp.concatenate([d_ref[0 : rows // 2, :], d_ref[rows // 2 : rows, :]], axis=1)
    ag[s] = a_ref[...]
    peers = chips + jnp.where(s > 0, 1, 0) + jnp.where(s < n - 1, 1, 0)
    pl.semaphore_wait(barrier, peers)

    kinds = 5
    reach = (far, far) + (min(2, far),) * 3

    def part_of(which, slab):
        if which < 3:
            return (cg, tg, dg)[which].at[slab]
        return ag.at[slab, pl.ds((which - 3) * (rows // 2), rows // 2)]

    def valid(e):
        return (s + e >= 0) & (s + e < n)

    def copy(way, step, which, slab):
        return pltpu.make_async_remote_copy(
            src_ref=part_of(which, slab),
            dst_ref=part_of(which, slab),
            send_sem=send_sem.at[way, step, which],
            recv_sem=recv_sem.at[way, step, which],
            device_id=(s + 1 if way == 0 else s - 1, p),
            device_id_type=MESH,
        )

    def send(way, step, which, act):
        if step >= reach[which]:
            return
        slab = s - step if way == 0 else s + step
        ok = valid(-step) & valid(1) if way == 0 else valid(step) & valid(-1)

        @pl.when(ok)
        def _():
            act(copy(way, step, which, slab))

    def start(c):
        c.start()

    def take(e, which):
        if abs(e) > reach[which]:
            return
        way, step = (0 if e < 0 else 1), abs(e) - 1

        @pl.when(valid(e))
        def _():
            copy(way, step, which, s + e).wait_recv()

        send(way, step + 1, which, start)

    for which in range(kinds):
        for way in range(2):
            send(way, 0, which, start)

    lane = lax.broadcasted_iota(jnp.int32, (tile, pair), 1) // tile
    lane_f = lane.astype(F32)

    def basis(e):
        @pl.when(valid(e))
        def _():
            u = s + e
            names = cg[u].astype(F32)
            for b in range(blocks):
                x = tg[u, b * tile : (b + 1) * tile, :].astype(F32)
                turned = pltpu.roll(x, tile, 1)
                two_t = jnp.where(lane == 0, turned, x)
                one_t = jnp.where(lane == 0, x, turned)
                g1 = jnp.broadcast_to(names[slots : slots + 1, b : b + 1], (1, pair))
                for q in range(w // pair):
                    ts[u, b * tile : (b + 1) * tile, q * pair : (q + 1) * pair] = jnp.where(
                        lane_f + 2.0 * q == g1, one_t, 0.0
                    ).astype(BF16)
                g2 = jnp.broadcast_to(names[slots + 1 : slots + 2, b : b + 1], (1, pair))
                for q in range(gw // pair):
                    t2s[u, b * tile : (b + 1) * tile, q * pair : (q + 1) * pair] = jnp.where(
                        lane_f + 2.0 * q == g2, two_t, 0.0
                    ).astype(BF16)

    def build(e, h):
        lo, hi = h * half * tile, (h + 1) * half * tile

        @pl.when(valid(e))
        def _():
            u = s + e
            if h == 0:
                codes = cg[u].astype(F32)
                at = lax.broadcasted_iota(jnp.int32, (slots, pair), 1) // tile
                at = at.astype(F32)
                for i in range(blocks):
                    code = jnp.broadcast_to(codes[0:slots, i : i + 1], (slots, pair))
                    for cp in range(3 * rows // pair):
                        hot[i, :, cp * pair : (cp + 1) * pair] = jnp.where(
                            code == at + 2.0 * cp, 1.0, 0.0
                        )

            def row(i, carry):
                base = pl.multiple_of(i * tile, tile)
                tiles = []
                for k2 in range(slots // 2):
                    x = ag[u, pl.ds(base, tile), k2 * pair : (k2 + 1) * pair].astype(F32)
                    turned = pltpu.roll(x, tile, 1)
                    for y in (jnp.where(lane == 0, x, turned), jnp.where(lane == 0, turned, x)):
                        tiles.append(y.astype(BF16).reshape(tile // 16, 16, pair))
                for cp in range(3 * rows // pair):
                    total = None
                    for k in range(slots):
                        m = hot[i, k : k + 1, cp * pair : (cp + 1) * pair]
                        m = jnp.broadcast_to(m, (16, pair)).astype(BF16)
                        y = tiles[k] * m[None]
                        total = y if total is None else total + y
                    ad[e + 2, pl.ds(base, tile), cp * pair : (cp + 1) * pair] = total.reshape(tile, pair)
                return carry

            lax.fori_loop(h * half, (h + 1) * half, row, 0)
            for b in range(half):
                x = dg[u, b * tile : (b + 1) * tile, :].astype(F32)
                if b % 2 != h:
                    x = pltpu.roll(x, tile, 1)
                bd[b * tile : (b + 1) * tile, (b // 2) * pair : (b // 2 + 1) * pair] = (
                    jnp.where(lane == b % 2, x, 0.0).astype(BF16)
                )
            sd[lo:hi, :] = (DAMPING * mm(bd[...], ad[e + 2, lo:hi, :])).astype(BF16)

        if abs(e) < 2:

            @pl.when(jnp.logical_not(valid(e)))
            def _():
                ad[e + 2, lo:hi, :] = jnp.zeros((hi - lo, 3 * rows), BF16)

    def prolong(e, j, lo, hi):
        ok = valid(e) & valid(e + j - 1)

        @pl.when(ok)
        def _():
            v = s + e + j - 1
            value = -mm(sd[lo:hi, j * rows : (j + 1) * rows], ts[v])
            if j == 1:
                value = value + ts[v, lo:hi, :].astype(F32)
            pro[e + 2, lo:hi, j * w : (j + 1) * w] = value.astype(BF16)

        @pl.when(jnp.logical_not(ok))
        def _():
            pro[e + 2, lo:hi, j * w : (j + 1) * w] = jnp.zeros((hi - lo, w), BF16)

    def pair_copy(m):
        return pltpu.make_async_remote_copy(
            src_ref=term.at[m, 1 - odd],
            dst_ref=rx1.at[m],
            send_sem=send1.at[m],
            recv_sem=recv1.at[m],
            device_id=(s, sibling),
            device_id_type=MESH,
        )

    def chip_copy(m, o):
        return pltpu.make_async_remote_copy(
            src_ref=tx2.at[m, o - 1],
            dst_ref=rx2.at[m, o - 1],
            send_sem=send2.at[m, o - 1],
            recv_sem=recv2.at[m, o - 1],
            device_id=(s, mates[o - 1]),
            device_id_type=MESH,
        )

    def leave(f):
        return pltpu.make_async_copy(
            cf.at[f + 3], out.at[s + f if n < 7 else f + 3], out_sem.at[f + 3]
        )

    def sum_over(f, sides):
        total = None
        for e in sides:
            j = f - e + 1
            part = mm(wm[e + 2], pro[e + 2, :, j * w : (j + 1) * w])
            total = part if total is None else total + part
        return total

    def early(f):
        sides = [e for e in (-1, 0, 1) if abs(f - e) < 2]

        @pl.when(valid(f))
        def _():
            cf[f + 3] = sum_over(f, sides)

    def coarse(f):
        m = f + 3

        @pl.when(valid(f))
        def _():
            if abs(f) == 3:
                cf[m] = sum_over(f, [2 if f > 0 else -2])
            elif f != 0:
                cf[m] += sum_over(f, [2 if f > 0 else -2])
            leave(f).start()
            left = mm(t2t[...], cf[m].astype(BF16)).astype(BF16)
            both = mm(left, t2s[s + f]).astype(BF16)
            for g in range(groups):
                term[m, g % 2, g // 2] = both[g * tile : (g + 1) * tile, :]
            pair_copy(m).start()

    def pair_sum(f):
        m = f + 3

        @pl.when(valid(f))
        def _():
            pair_copy(m).wait_recv()
            for o in range(1, chips):
                h = lax.rem(chip + o, chips)
                tx2[m, o - 1] = (term[m, odd, h].astype(F32) + rx1[m, h].astype(F32)).astype(BF16)
                chip_copy(m, o).start()
            mine[m] = term[m, odd, chip].astype(F32) + rx1[m, chip].astype(F32)

    bd[...] = jnp.zeros_like(bd)
    for f in range(-3, 4):

        @pl.when(jnp.logical_not(valid(f)))
        def _(f=f):
            two[:, (f + 3) * gw : (f + 4) * gw] = jnp.zeros((tile, gw), F32)

    basis(0)
    t2t[...] = t2s[s].astype(F32).T.astype(BF16)
    build(0, 0)
    build(0, 1)
    for e in (-1, 1):
        take(e, 0)
        take(e, 1)
        basis(e)
    for j in range(3):
        prolong(0, j, 0, rows)
    for h in range(2):
        for e in (-1, 1):
            if h == 0:
                take(e, 2)
            take(e, 3 + h)
    for e in (-2, 2):
        take(e, 0)
        take(e, 1)
        basis(e)
    for e in (-1, 1):
        build(e, 0)
        build(e, 1)
        for j in range(3):
            prolong(e, j, 0, rows)
    turned = [
        pro[dj + 2, :, (1 - dj) * w : (2 - dj) * w].astype(F32).T.astype(BF16) for dj in (-1, 0, 1)
    ]
    for e in range(-2, 3):
        total = None
        for dj in (-1, 0, 1):
            j = e - dj + 1
            if 0 <= j < 3:
                part = mm(turned[dj + 1], ad[dj + 2, :, j * rows : (j + 1) * rows])
                total = part if total is None else total + part
        wm[e + 2] = total.astype(BF16)
    early(0)
    coarse(0)
    for f in (-2, -1, 1, 2):
        early(f)
    pair_sum(0)
    for e in (-3, 3):
        take(e, 0)
        take(e, 1)
        basis(e)
    order = [0]
    for way in (-1, 1):
        e = 2 * way
        take(e, 2)
        take(e, 3)
        build(e, 0)
        for j in range(3):
            prolong(e, j, 0, rows // 2)
        take(e, 4)
        build(e, 1)
        for f in (way, 2 * way, 3 * way):
            prolong(e, f - e + 1, rows // 2, rows)
            coarse(f)
            if order[-1] != 0:
                pair_sum(order[-1])
            order.append(f)
    pair_sum(order[-1])
    for f in order:
        m = f + 3

        @pl.when(valid(f))
        def _(m=m):
            total = mine[m]
            for o in range(1, chips):
                chip_copy(m, o).wait_recv()
                total = total + rx2[m, o - 1].astype(F32)
            two[:, m * gw : (m + 1) * gw] = total

    for f in range(-3, 4):
        m = f + 3

        @pl.when(valid(f))
        def _(f=f, m=m):
            leave(f).wait()
            pair_copy(m).wait_send()
            for o in range(1, chips):
                chip_copy(m, o).wait_send()

    for step in range(far):
        for which in range(kinds):
            for way in range(2):
                send(way, step, which, lambda c: c.wait_send())


def place_kernel(n, blocks, level, out, two, zero, sem, last):
    s = lax.axis_index("slab")
    cut, w = zero.shape
    parts = w // cut
    other = pltpu.make_async_copy(level, two, last)
    other.start()
    zero[...] = jnp.zeros_like(zero)

    def each(act):
        for f in range(-3, 4):
            ok = (s + f >= 0) & (s + f < n)
            for q in range(parts):
                to = out.at[pl.ds(q * cut, cut), pl.ds((f + 3) * w, w)]

                @pl.when(ok)
                def _(f=f, q=q, to=to):
                    slab = s + f if n < 7 else f + 3
                    have = blocks.at[slab, pl.ds(q * cut, cut)]
                    act(pltpu.make_async_copy(have, to, sem.at[f + 3, q]))

                @pl.when(jnp.logical_not(ok))
                def _(f=f, q=q, to=to):
                    act(pltpu.make_async_copy(zero, to, sem.at[f + 3, q]))

    each(lambda c: c.start())
    each(lambda c: c.wait())
    other.wait()


def at_once(
    fine_tiles, fine_cols, bond_mask, diag_inv, tentative, aggregate, tentative_two, aggregate_two
):
    blocks, tile = diag_inv.shape[0], diag_inv.shape[1]
    slots = fine_cols.shape[1]
    aggs = tentative_two.shape[0]
    n, groups = lax.axis_size("slab"), lax.axis_size("piece")
    rows, w, gw = blocks * tile, aggs * tile, groups * tile
    pair, chips, far = 2 * tile, groups // 2, min(3, n - 1)
    names = -(-(slots + 2) // 16) * 16
    kept = min(n, 7)
    vmem = pl.BlockSpec(memory_space=pltpu.VMEM)
    smem = pl.BlockSpec(memory_space=pltpu.SMEM)
    dma = pltpu.SemaphoreType.DMA
    scratch = [
        pltpu.VMEM((n, rows, slots * tile), BF16),
        pltpu.VMEM((n, rows // 2, pair), BF16),
        pltpu.VMEM((n, rows, pair), BF16),
        pltpu.VMEM((n, names, LANES), BF16),
        pltpu.VMEM((5, rows, 3 * rows), BF16),
        pltpu.VMEM((rows, 3 * rows), BF16),
        pltpu.VMEM((5, rows, 3 * w), BF16),
        pltpu.VMEM((n, rows, w), BF16),
        pltpu.VMEM((n, w, gw), BF16),
        pltpu.VMEM((gw, w), BF16),
        pltpu.VMEM((blocks, slots, 3 * rows), F32),
        pltpu.VMEM((rows // 2, rows // 2), BF16),
        pltpu.VMEM((5, w, rows), BF16),
        pltpu.VMEM((7, w, w), F32),
        pltpu.VMEM((7, 2, chips, tile, gw), BF16),
        pltpu.VMEM((7, tile, gw), F32),
        pltpu.VMEM((7, chips, tile, gw), BF16),
        pltpu.VMEM((7, chips - 1, tile, gw), BF16),
        pltpu.VMEM((7, chips - 1, tile, gw), BF16),
    ]
    size = sum(x.dtype.itemsize * np.prod(x.shape) for x in scratch)
    if size > 0.92 * FUSED_LIMIT:
        return None
    held, level_two = pl.pallas_call(
        functools.partial(whole_kernel, n, blocks, slots, aggs, groups, tile),
        out_shape=(
            jax.ShapeDtypeStruct((kept, w, w), F32),
            jax.ShapeDtypeStruct((tile, 7 * gw), F32),
        ),
        in_specs=[vmem] * 4 + [smem] * 4,
        out_specs=(pl.BlockSpec(memory_space=pl.ANY), vmem),
        scratch_shapes=scratch
        + [
            dma((2, far, 5)),
            dma((2, far, 5)),
            dma((7,)),
            dma((7,)),
            dma((7,)),
            dma((7, chips - 1)),
            dma((7, chips - 1)),
        ],
        compiler_params=pltpu.CompilerParams(
            collective_id=2, has_side_effects=True, vmem_limit_bytes=VMEM_LIMIT
        ),
    )(
        fine_tiles.reshape(rows, slots * tile),
        diag_inv.reshape(rows, tile),
        tentative.reshape(rows, tile),
        tentative_two.reshape(w, tile),
        fine_cols,
        bond_mask,
        aggregate,
        aggregate_two,
    )
    coarse, level_two = pl.pallas_call(
        functools.partial(place_kernel, n),
        out_shape=(
            jax.ShapeDtypeStruct((w, 7 * w), F32),
            jax.ShapeDtypeStruct((tile, 7 * gw), F32),
        ),
        in_specs=[pl.BlockSpec(memory_space=pl.ANY)] * 2,
        out_specs=(pl.BlockSpec(memory_space=pl.ANY),) * 2,
        scratch_shapes=[
            pltpu.VMEM((w // 4, w), F32),
            dma((7, 4)),
            dma(()),
        ],
        compiler_params=pltpu.CompilerParams(vmem_limit_bytes=4 * 1024 * 1024),
    )(held, level_two)
    return (coarse.reshape(aggs, tile, 7 * w), level_two.reshape(1, tile, 7 * gw))


def per_device(*args):
    done = at_once(*args)
    return in_stages(*args) if done is None else done


def solution(mesh):
    placed = (
        P(("slab", "piece"), None, None),
        P(("slab", "piece"), None),
        P(("slab", "piece"), None),
        P(("slab", "piece"), None, None),
        P(("slab", "piece"), None, None),
        P(("slab", "piece")),
        P(("slab", "piece"), None, None),
        P(("slab", "piece")),
    )
    return jax.shard_map(
        per_device,
        mesh=mesh,
        in_specs=placed,
        out_specs=(P(("slab", "piece"), None, None), P(("slab", "piece"), None, None)),
        check_vma=False,
    )
```
